512 devices in a mesh: lat: 16 (over x, z_lo, core), lon: 32 (over y, z_hi).
Axes of the slice: x: 4, y: 8, z: 8 (z_hi: 4, z_lo: 2; z = z_hi * 2 + z_lo), core: 2. Of those that a mesh axis runs over, the one named last changes fastest.
Arguments:
- field: bfloat16 [1440, 720, 256], P('lon', 'lat'), may hold values from -6 to 6
- cotangent: bfloat16 [1440, 720, 256], P('lon', 'lat'), may hold values from -6 to 6
- spectral_filter: bfloat16 [2, 720, 256], P(None, None, 'lon'), may hold values from -4 to 4
Outputs:
- output: bfloat16 [1440, 720, 256], P('lon', 'lat')
- grad_field: bfloat16 [1440, 720, 256], P('lon', 'lat')
- grad_filter: float32 [2, 720, 256], P(None, None, 'lon')
The draws below stay inside these ranges and needn't reach their ends.
All inputs are finite; a program needn't handle non-finite values.
Results may differ from the reference program's by a relative error of at most 0.024.
Values may be sent and summed in bfloat16 or wider, within the bound.
No kernel may reach another device: no remote copies, remote signals or barrier semaphores. Data moves between devices by JAX's collectives and lax.ppermute only.
A program may use at most 128 MiB of HBM per device.

```python
import math
import jax
import jax.numpy as jnp
from jax import lax

C = 256
NLAT = 720
NLON = 1440
L = 720
M = 512


def shard_levels(key, shape, cuts, low, top_value):
    def one(position, parts):
        draws = jax.random.uniform(jax.random.fold_in(jax.random.fold_in(key, 6), position), (parts,), jnp.float32, low / len(cuts), top_value / len(cuts))
        return jnp.repeat(jnp.exp(draws), shape[position] // parts).reshape((-1,) + (1,) * (len(shape) - position - 1))

    factor_of = one(*cuts[0])
    for cut in cuts[1:]:
        factor_of = factor_of * one(*cut)
    return factor_of


def bell_draw(stream_key, dims, deviation, most, split=(), kind=jnp.bfloat16):
    drawn = deviation * jax.random.normal(stream_key, dims, jnp.float32)
    if split:
        drawn = drawn * shard_levels(stream_key, dims, split, -0.22, 0.18)
    return jnp.clip(drawn, -most, most).astype(kind)


def setup_inputs(seed: int = 0) -> dict:
    key_list = jax.random.split(jax.random.key(seed), 4)
    return {
        "field": bell_draw(key_list[0], (NLON, NLAT, C), 1.0, 6.0, ((0, 32), (1, 16))),
        "cotangent": bell_draw(key_list[1], (NLON, NLAT, C), 1.0, 6.0, ((0, 32), (1, 16))),
        "spectral_filter": bell_draw(key_list[2], (2, L, C), 0.7, 4.0, ((2, 32),)),
    }


def fourier_table(wave_count, points):
    wave_index = jnp.arange(wave_count, dtype=jnp.int32)
    point_index = jnp.arange(points, dtype=jnp.int32)
    phase_steps = wave_index[:, None] * point_index[None, :] % points
    angles = phase_steps.astype(jnp.float32) * (2.0 * math.pi / points)
    stacked = jnp.stack([jnp.cos(angles), -jnp.sin(angles)], axis=1)
    return stacked.reshape(2 * wave_count, points).astype(jnp.bfloat16)

def compose(earlier, latter):
    upper_left = latter[0] * earlier[0] + latter[1] * earlier[2]
    upper_right = latter[0] * earlier[1] + latter[1] * earlier[3]
    lower_left = latter[2] * earlier[0] + latter[3] * earlier[2]
    lower_right = latter[2] * earlier[1] + latter[3] * earlier[3]
    largest = jnp.maximum(jnp.maximum(jnp.abs(upper_left), jnp.abs(upper_right)), jnp.maximum(jnp.abs(lower_left), jnp.abs(lower_right)))
    return (upper_left / largest, upper_right / largest, lower_left / largest, lower_right / largest, earlier[4] + latter[4] + jnp.log(largest))

def legendre_pair(wave_order, lat_count, degree_count):
    order_value = wave_order.astype(jnp.float32)
    degrees = jnp.arange(degree_count, dtype=jnp.float32)
    beyond = degrees > order_value
    numerator = jnp.where(beyond, 4.0 * degrees * degrees - 1.0, 1.0)
    denominator = jnp.where(beyond, degrees * degrees - order_value * order_value, 1.0)
    factor = jnp.sqrt(numerator / denominator)
    earlier_factor = jnp.concatenate([jnp.ones((1,), jnp.float32), factor[:-1]])
    subdiagonal = jnp.where(degrees > order_value + 1.0, -factor / earlier_factor, 0.0)
    start_log = 0.5 * (lax.lgamma(order_value + 1.5) - lax.lgamma(jnp.float32(1.5)) - lax.lgamma(order_value + 1.0)) - 0.5 * math.log(4.0 * math.pi)
    colatitude = (jnp.arange(lat_count, dtype=jnp.float32) + 0.5) * (math.pi / lat_count)
    cosine = jnp.cos(colatitude)[None, :]
    sines = jnp.sin(colatitude)
    block_len = 16
    block_count = degree_count // block_len
    grid_shape = (block_count, lat_count)

    def picked(values, step):
        return values.reshape(block_count, block_len)[:, step][:, None]

    def element(step):
        inside = picked(beyond, step)
        return (jnp.where(inside, 0.0, 1.0).astype(jnp.float32), jnp.where(inside, 1.0, 0.0).astype(jnp.float32), picked(subdiagonal, step).astype(jnp.float32), jnp.where(inside, picked(factor, step) * cosine, 1.0).astype(jnp.float32), jnp.zeros((block_count, 1), jnp.float32))
    ones_grid = jnp.ones(grid_shape, jnp.float32)
    zeros_grid = jnp.zeros(grid_shape, jnp.float32)
    identity = (ones_grid, zeros_grid, zeros_grid, ones_grid, zeros_grid)
    totals = identity
    for step in range(block_len):
        totals = compose(totals, element(step))
    inclusive = lax.associative_scan(compose, totals, axis=0)
    carry = tuple((jnp.concatenate([first[:1], later[:-1]], axis=0) for first, later in zip(identity, inclusive)))
    lower_parts = []
    log_parts = []
    for step in range(block_len):
        carry = compose(carry, element(step))
        lower_parts.append(carry[3])
        log_parts.append(carry[4])
    lower_right = jnp.stack(lower_parts, axis=1).reshape(degree_count, lat_count)
    log_scale = jnp.stack(log_parts, axis=1).reshape(degree_count, lat_count)
    values = lower_right * jnp.exp(log_scale + start_log + order_value * jnp.log(sines)[None, :])
    functions = jnp.where((degrees >= order_value)[:, None], values, 0.0)
    weights = math.pi / lat_count * sines
    return (functions.astype(jnp.bfloat16), (functions * weights[None, :]).astype(jnp.bfloat16))

def spectral_products(weights, analysis, adjoint_synthesis):
    filter_real = weights[0]
    filter_imaginary = weights[1]
    real_part = filter_real * analysis[0] - filter_imaginary * analysis[1]
    imaginary_part = filter_real * analysis[1] + filter_imaginary * analysis[0]
    filtered = jnp.stack([real_part, imaginary_part]).astype(jnp.bfloat16)
    gradient_term = jnp.stack([analysis[0] * adjoint_synthesis[0] + analysis[1] * adjoint_synthesis[1], analysis[0] * adjoint_synthesis[1] - analysis[1] * adjoint_synthesis[0]])
    adjoint_filtered = jnp.stack([filter_real * adjoint_synthesis[0] + filter_imaginary * adjoint_synthesis[1], filter_real * adjoint_synthesis[1] - filter_imaginary * adjoint_synthesis[0]]).astype(jnp.bfloat16)
    return (filtered, gradient_term, adjoint_filtered)

def reference(field, cotangent, spectral_filter):
    highest = lax.Precision.HIGHEST
    fourier_rows = fourier_table(M, NLON).astype(jnp.float32)
    spacing = 2.0 * math.pi / NLON
    doubling = jnp.where(jnp.arange(2 * M) // 2 == 0, 1.0, 2.0).astype(jnp.float32)[:, None]
    weights = spectral_filter.astype(jnp.float32)

    def analyze(lat_row):
        return (jnp.dot(fourier_rows, lat_row.astype(jnp.float32), precision=highest) * spacing).astype(jnp.bfloat16)

    def adjoint_in(lat_row):
        return (jnp.dot(fourier_rows, lat_row.astype(jnp.float32), precision=highest) * doubling).astype(jnp.bfloat16)
    fourier = lax.map(analyze, jnp.transpose(field, (1, 0, 2)))
    adjoint_fourier = lax.map(adjoint_in, jnp.transpose(cotangent, (1, 0, 2)))
    fourier_modes = jnp.transpose(fourier.reshape(NLAT, M, 2, C), (1, 2, 0, 3))
    adjoint_modes = jnp.transpose(adjoint_fourier.reshape(NLAT, M, 2, C), (1, 2, 0, 3))

    def per_order(running, inputs):
        wave_order, fourier_spec, adjoint_spec = inputs
        legendre, weighted = legendre_pair(wave_order, NLAT, L)
        legendre = legendre.astype(jnp.float32)
        weighted = weighted.astype(jnp.float32)
        analysis = jnp.einsum('lj,rjc->rlc', weighted, fourier_spec.astype(jnp.float32), precision=highest)
        adjoint_synthesis = jnp.einsum('lj,rjc->rlc', legendre, adjoint_spec.astype(jnp.float32), precision=highest)
        filtered, gradient_term, adjoint_filtered = spectral_products(weights, analysis, adjoint_synthesis)
        synthesis = jnp.einsum('lj,rlc->rjc', legendre, filtered.astype(jnp.float32), precision=highest).astype(jnp.bfloat16)
        adjoint_analysis = jnp.einsum('lj,rlc->rjc', weighted, adjoint_filtered.astype(jnp.float32), precision=highest).astype(jnp.bfloat16)
        return (running + gradient_term, (synthesis, adjoint_analysis))
    grad_filter, (synthesis_modes, adjoint_modes_back) = lax.scan(per_order, jnp.zeros((2, L, C), jnp.float32), (jnp.arange(M, dtype=jnp.int32), fourier_modes, adjoint_modes))
    synthesis_rows = jnp.transpose(synthesis_modes, (2, 0, 1, 3)).reshape(NLAT, 2 * M, C)
    adjoint_rows = jnp.transpose(adjoint_modes_back, (2, 0, 1, 3)).reshape(NLAT, 2 * M, C)

    def synthesize(lat_row):
        return jnp.dot(fourier_rows.T, doubling * lat_row.astype(jnp.float32), precision=highest).astype(jnp.bfloat16)

    def adjoint_out(lat_row):
        return (jnp.dot(fourier_rows.T, lat_row.astype(jnp.float32), precision=highest) * spacing).astype(jnp.bfloat16)
    output = jnp.transpose(lax.map(synthesize, synthesis_rows), (1, 0, 2))
    grad_field = jnp.transpose(lax.map(adjoint_out, adjoint_rows), (1, 0, 2))
    return (output, grad_field, grad_filter)
```

```python
import functools
import math

import jax
import jax.numpy as jnp
from jax import lax
from jax.experimental import pallas as pl
from jax.experimental.pallas import tpu as pltpu
from jax.sharding import PartitionSpec as P

LAT, LON = 16, 32
NLOC, JLOC = 45, 45
NPAD, JPAD = 48, 48
CH = 8
NT = NPAD // 16
KDIM = LON * NPAD
MUDIM = 1024
GROUPS, TG = 4, 8
JALL = LAT * JPAD
DEG, LPAD = 720, 768
POINTS = NLOC * LON
F32, BF16 = jnp.float32, jnp.bfloat16
MIB = 1 << 20


def exchange(tiles, tile_bit, lane_bit):
    step = 1 << lane_bit
    lane = lax.broadcasted_iota(jnp.int32, tiles[0].shape, 1)
    low = (lane & step) == 0
    out = list(tiles)
    for first in range(len(tiles)):
        second = first | (1 << tile_bit)
        if second == first:
            continue
        a, b = tiles[first], tiles[second]
        out[first] = jnp.where(low, a, pltpu.roll(b, step, 1))
        out[second] = jnp.where(low, pltpu.roll(a, 128 - step, 1), b)
    return out


def cost(flops, size):
    return pl.CostEstimate(flops=int(flops), bytes_accessed=int(size), transcendentals=0)


def params(mib):
    return pltpu.CompilerParams(vmem_limit_bytes=mib * MIB)


def share_kernel(x_ref, o_ref):
    def body(nt, jr):
        rows = pl.ds(pl.multiple_of(jr * 16, 16), 16)
        for h in range(2):
            tiles = [
                x_ref[nt * 16 + n, rows, h * 128 : h * 128 + 128].astype(F32) for n in range(16)
            ]
            for b in range(4):
                tiles = exchange(tiles, b, 3 + b)
            for k in range(16):
                o_ref[h * 16 + k, nt, rows, :] = tiles[k].astype(BF16)

    @pl.loop(0, NT * 3)
    def _(s):
        body(s // 3, s % 3)


def to_shares(grid):
    padded = jnp.pad(grid, ((0, NPAD - NLOC), (0, JPAD - JLOC), (0, 0)))
    return pl.pallas_call(
        share_kernel,
        out_shape=jax.ShapeDtypeStruct((LON, NT, JPAD, 128), BF16),
        in_specs=[pl.BlockSpec(memory_space=pltpu.VMEM)],
        out_specs=pl.BlockSpec(memory_space=pltpu.VMEM),
        compiler_params=params(32),
        cost_estimate=cost(1e7, 2.4e6),
        name="to_shares",
    )(padded)


def unshare_kernel(x_ref, o_ref):
    for nt in range(NT):
        for jr in range(3):
            rows = pl.ds(jr * 16, 16)
            count = min(16, JLOC - jr * 16)
            for h in range(2):
                tiles = [x_ref[h * 16 + k, nt, rows, :].astype(F32) for k in range(16)]
                for b in range(4):
                    tiles = exchange(tiles, b, 3 + b)
                for n in range(min(16, NLOC - nt * 16)):
                    o_ref[nt * 16 + n, jr * 16 : jr * 16 + count, h * 128 : h * 128 + 128] = (
                        tiles[n].astype(BF16)[:count]
                    )


def from_shares(shares):
    return pl.pallas_call(
        unshare_kernel,
        out_shape=jax.ShapeDtypeStruct((NLOC, JLOC, 256), BF16),
        in_specs=[pl.BlockSpec(memory_space=pltpu.VMEM)],
        out_specs=pl.BlockSpec(memory_space=pltpu.VMEM),
        compiler_params=params(32),
        cost_estimate=cost(1e7, 2.4e6),
        name="from_shares",
    )(shares)


def fourier_kernel(x_ref, f_ref, row_ref, lane_ref, o_ref, xs_ref, ys_ref):
    @pl.loop(0, 3 * (KDIM // 128))
    def _(s):
        jr, q8 = s // (KDIM // 128), s % (KDIM // 128)
        rows = pl.ds(pl.multiple_of(jr * 16, 16), 16)
        tiles = [x_ref[q8 * 8 + q, rows, :].astype(F32) for q in range(8)]
        for b in range(3):
            tiles = exchange(tiles, b, b)
        lanes = pl.ds(pl.multiple_of(q8 * 128, 128), 128)
        for c in range(8):
            xs_ref[pl.ds(pl.multiple_of(jr * 128 + c * 16, 16), 16), lanes] = tiles[c].astype(BF16)

    ys_ref[...] = jnp.dot(xs_ref[...], f_ref[...], preferred_element_type=F32)

    @pl.loop(0, 3 * 8)
    def _(s):
        jr, ii = s // 8, s % 8
        rows = pl.ds(pl.multiple_of(jr * 16, 16), 16)
        lanes = pl.ds(pl.multiple_of(ii * 128, 128), 128)
        scale = row_ref[rows, :] * lane_ref[:, lanes]
        tiles = [
            ys_ref[pl.ds(pl.multiple_of(jr * 128 + c * 16, 16), 16), lanes] * scale
            for c in range(8)
        ]
        for b in range(3):
            tiles = exchange(tiles, b, 4 + b)
        for i_lo in range(2):
            for g in range(GROUPS):
                o_ref[ii * 2 + i_lo, g, rows, :] = tiles[i_lo * 4 + g].astype(BF16)


def to_waves(shares, table, row_scale, lane_scale):
    return pl.pallas_call(
        fourier_kernel,
        out_shape=jax.ShapeDtypeStruct((LAT, GROUPS, JPAD, 128), BF16),
        in_specs=[pl.BlockSpec(memory_space=pltpu.VMEM)] * 4,
        out_specs=pl.BlockSpec(memory_space=pltpu.VMEM),
        scratch_shapes=[
            pltpu.VMEM((CH * JPAD, KDIM), BF16),
            pltpu.VMEM((CH * JPAD, MUDIM), F32),
        ],
        compiler_params=params(32),
        cost_estimate=cost(2 * 384 * KDIM * MUDIM, 5e6),
        name="to_waves",
    )(shares.reshape(LON * NT, JPAD, 128), table, row_scale, lane_scale)


def inverse_kernel(v_ref, f_ref, row_ref, lane_ref, o_ref, vs_ref, ys_ref):
    @pl.loop(0, 3 * 8)
    def _(s):
        jr, ii = s // 8, s % 8
        rows = pl.ds(pl.multiple_of(jr * 16, 16), 16)
        lanes = pl.ds(pl.multiple_of(ii * 128, 128), 128)
        tiles = [
            v_ref[ii * 2 + i_lo, g, rows, :].astype(F32) for i_lo in range(2) for g in range(GROUPS)
        ]
        for b in range(3):
            tiles = exchange(tiles, b, 4 + b)
        scale = lane_ref[:, lanes]
        for c in range(8):
            vs_ref[pl.ds(pl.multiple_of(jr * 128 + c * 16, 16), 16), lanes] = (
                tiles[c] * scale
            ).astype(BF16)

    ys_ref[...] = lax.dot_general(
        vs_ref[...], f_ref[...], (((1,), (1,)), ((), ())), preferred_element_type=F32
    )

    @pl.loop(0, 3 * (KDIM // 128))
    def _(s):
        jr, q8 = s // (KDIM // 128), s % (KDIM // 128)
        rows = pl.ds(pl.multiple_of(jr * 16, 16), 16)
        lanes = pl.ds(pl.multiple_of(q8 * 128, 128), 128)
        scale = row_ref[rows, :]
        tiles = [
            ys_ref[pl.ds(pl.multiple_of(jr * 128 + c * 16, 16), 16), lanes] * scale
            for c in range(8)
        ]
        for b in range(3):
            tiles = exchange(tiles, b, b)
        for q in range(8):
            o_ref[q8 * 8 + q, rows, :] = tiles[q].astype(BF16)


def from_waves(waves, table, row_scale, lane_scale):
    return pl.pallas_call(
        inverse_kernel,
        out_shape=jax.ShapeDtypeStruct((LON * NT, JPAD, 128), BF16),
        in_specs=[pl.BlockSpec(memory_space=pltpu.VMEM)] * 4,
        out_specs=pl.BlockSpec(memory_space=pltpu.VMEM),
        scratch_shapes=[
            pltpu.VMEM((CH * JPAD, MUDIM), BF16),
            pltpu.VMEM((CH * JPAD, KDIM), F32),
        ],
        compiler_params=params(32),
        cost_estimate=cost(2 * 384 * KDIM * MUDIM, 5e6),
        name="from_waves",
    )(waves, table, row_scale, lane_scale).reshape(LON, NT, JPAD, 128)


LCHUNK = 128


def legendre_kernel(m_ref, f_ref, h_ref, x_ref, p0_ref, e0_ref, o_ref, p1_s, p2_s, e_s, rows_s):
    g, lc = pl.program_id(0), pl.program_id(1)

    @pl.when(lc == 0)
    def _():
        p1_s[...] = jnp.zeros_like(p1_s)
        p2_s[...] = jnp.zeros_like(p2_s)
        e_s[...] = e0_ref[0]

    @pl.when(lc < g)
    def _():
        o_ref[...] = jnp.zeros_like(o_ref)

    @pl.when(lc >= g)
    def _():
        x = jnp.broadcast_to(x_ref[...], (TG, JALL))
        orders = jnp.broadcast_to(m_ref[0][:, :1], (TG, JALL))

        def block(s, carry):
            p1, p2, e = carry
            shift = lax.rem(LCHUNK - s * 16, LCHUNK)
            fs = pltpu.roll(f_ref[0], shift, 1)
            hs = pltpu.roll(h_ref[0], shift, 1)
            for u in range(16):
                if u % 8 == 0:
                    big = jnp.abs(p1) > 2.0**24
                    p1 = jnp.where(big, p1 * 2.0**-48, p1)
                    p2 = jnp.where(big, p2 * 2.0**-48, p2)
                    e = jnp.where(big, e + 48.0, e)
                    scale = jnp.exp2(jnp.maximum(e, -200.0))
                degree = (lc * LCHUNK + s * 16 + u).astype(F32)
                step = (fs[:, u : u + 1] * x) * p1 - hs[:, u : u + 1] * p2
                new = jnp.where(orders == degree, p0_ref[0], step)
                p1, p2 = new, p1
                value = new * scale
                for b in range(JALL // 128):
                    rows_s[b, pl.ds(pl.multiple_of((s * 16 + u) * TG, TG), TG), :] = value[
                        :, b * 128 : b * 128 + 128
                    ]
            return p1, p2, e

        p1, p2, e = lax.fori_loop(0, LCHUNK // 16, block, (p1_s[...], p2_s[...], e_s[...]))
        p1_s[...] = p1
        p2_s[...] = p2
        e_s[...] = e
        for t in range(TG):
            for b in range(JALL // 128):
                o_ref[t, :, b * 128 : b * 128 + 128] = rows_s[
                    b, pl.ds(t, LCHUNK, stride=TG), :
                ].astype(BF16)


def legendre_tables(lat):
    order = (lat + LAT * jnp.arange(GROUPS * TG, dtype=jnp.int32)).astype(F32)[:, None]
    degrees = jnp.arange(LPAD, dtype=F32)[None, :]

    def factor_at(degree):
        inside = degree > order
        top = jnp.where(inside, 4.0 * degree * degree - 1.0, 1.0)
        low = jnp.where(inside, degree * degree - order * order, 1.0)
        return jnp.sqrt(top / low), inside

    factor, inside = factor_at(degrees)
    earlier, earlier_inside = factor_at(degrees - 1.0)
    forward = jnp.where(inside, factor, 0.0).reshape(GROUPS, TG, LPAD)
    back = jnp.where(earlier_inside, factor / earlier, 0.0).reshape(GROUPS, TG, LPAD)
    start_log = 0.5 * (
        lax.lgamma(order + 1.5) - lax.lgamma(jnp.float32(1.5)) - lax.lgamma(order + 1.0)
    ) - 0.5 * math.log(4.0 * math.pi)
    place = jnp.arange(JALL, dtype=jnp.int32)
    cycle = place // JPAD * JLOC + jnp.minimum(place % JPAD, JLOC - 1)
    theta = (cycle.astype(F32) + 0.5) * (math.pi / (JLOC * LAT))
    start = (start_log + order * jnp.log(jnp.sin(theta))[None, :]) * (1.0 / math.log(2.0))
    exponent = jnp.floor(start)
    real = (place % JPAD < JLOC)[None, :]
    mantissa = jnp.where(real, jnp.exp2(start - exponent), 0.0)
    orders = jnp.broadcast_to(order, (GROUPS * TG, 128)).reshape(GROUPS, TG, 128)
    return pl.pallas_call(
        legendre_kernel,
        grid=(GROUPS, LPAD // LCHUNK),
        out_shape=jax.ShapeDtypeStruct((GROUPS * TG, LPAD, JALL), BF16),
        in_specs=[
            pl.BlockSpec((1, TG, 128), lambda g, lc: (g, 0, 0)),
            pl.BlockSpec((1, TG, LCHUNK), lambda g, lc: (g, 0, lc)),
            pl.BlockSpec((1, TG, LCHUNK), lambda g, lc: (g, 0, lc)),
            pl.BlockSpec((1, JALL), lambda g, lc: (0, 0)),
            pl.BlockSpec((1, TG, JALL), lambda g, lc: (g, 0, 0)),
            pl.BlockSpec((1, TG, JALL), lambda g, lc: (g, 0, 0)),
        ],
        out_specs=pl.BlockSpec((TG, LCHUNK, JALL), lambda g, lc: (g, lc, 0)),
        scratch_shapes=[pltpu.VMEM((TG, JALL), F32)] * 3 + [
            pltpu.VMEM((JALL // 128, LCHUNK * TG, 128), F32)
        ],
        compiler_params=params(32),
        cost_estimate=cost(2.5e10, 4e7),
        name="legendre_tables",
    )(
        orders,
        forward,
        back,
        jnp.cos(theta)[None, :],
        mantissa.reshape(GROUPS, TG, JALL),
        exponent.reshape(GROUPS, TG, JALL),
    )


def spectral_body(p_ref, z_ref, w_ref, sign, o_ref, s_ref, u_ref):
    z = z_ref[:, 0].reshape(JALL, 128).astype(F32)
    lane = lax.broadcasted_iota(jnp.int32, z.shape, 1) % TG
    for t in range(TG):
        part = jnp.dot(
            p_ref[t], jnp.where(lane == t, z, 0.0).astype(BF16), preferred_element_type=F32
        )
        s_ref[...] = part if t == 0 else s_ref[...] + part
    found = s_ref[...].T.reshape(CH, 2, TG, LPAD)
    real, imag = found[:, 0], found[:, 1]
    cross = w_ref[1] * sign
    kept = jnp.stack([w_ref[0] * real - cross * imag, w_ref[0] * imag + cross * real], axis=1)
    kept = kept.reshape(128, LPAD)
    row = lax.broadcasted_iota(jnp.int32, kept.shape, 0) % TG
    for t in range(TG):
        part = jnp.dot(
            jnp.where(row == t, kept, 0.0).astype(BF16), p_ref[t], preferred_element_type=F32
        )
        u_ref[...] = part if t == 0 else u_ref[...] + part
    o_ref[:, 0] = u_ref[...].T.astype(BF16).reshape(LAT, JPAD, 128)
    return real, imag


def forward_kernel(p_ref, z_ref, w_ref, o_ref, a_ref, s_ref, u_ref):
    real, imag = spectral_body(p_ref, z_ref, w_ref, 1.0, o_ref, s_ref, u_ref)
    a_ref[0, 0] = real
    a_ref[0, 1] = imag


def backward_kernel(p_ref, z_ref, w_ref, a_ref, o_ref, g_ref, s_ref, u_ref):
    real, imag = spectral_body(p_ref, z_ref, w_ref, -1.0, o_ref, s_ref, u_ref)
    first, second = a_ref[0, 0], a_ref[0, 1]

    @pl.when(pl.program_id(0) == 0)
    def _():
        g_ref[...] = jnp.zeros_like(g_ref)

    g_ref[0] += first * real + second * imag
    g_ref[1] += first * imag - second * real


def spectral_stage(kernel, tables, spectra, weights, extra_in, extra_out):
    wave_spec = pl.BlockSpec((LAT, 1, JPAD, 128), lambda g: (0, g, 0, 0))
    return pl.pallas_call(
        kernel,
        grid=(GROUPS,),
        out_shape=(jax.ShapeDtypeStruct((LAT, GROUPS, JPAD, 128), BF16), extra_out[0]),
        in_specs=[
            pl.BlockSpec((TG, LPAD, JALL), lambda g: (g, 0, 0)),
            wave_spec,
            pl.BlockSpec((2, CH, TG, LPAD), lambda g: (0, 0, 0, 0)),
        ]
        + [spec for _, spec in extra_in],
        out_specs=(wave_spec, extra_out[1]),
        scratch_shapes=[pltpu.VMEM((LPAD, 128), F32), pltpu.VMEM((128, JALL), F32)],
        compiler_params=params(48),
        cost_estimate=cost(1.2e10, 4.2e7),
        name="spectral_stage",
    )(tables, spectra, weights, *[value for value, _ in extra_in])


def fourier_table():
    kappa = jnp.arange(KDIM, dtype=jnp.int32)
    block = kappa // 128 * 8 + kappa % 8
    local = block % NT * 16 + kappa // 8 % 16
    point = (block // NT * NLOC + local)[:, None]
    real = (local < NLOC)[:, None]
    mu = jnp.arange(MUDIM, dtype=jnp.int32)
    lat = mu // 128 * 2 + mu // 64 % 2
    wave = (lat + LAT * (mu // 16 % 4 * TG + mu % TG))[None, :]
    quarter = (mu // 8 % 2 * (POINTS // 4))[None, :]
    phase = (wave * point + quarter) % POINTS
    values = jnp.cos(phase.astype(F32) * (2.0 * math.pi / POINTS))
    return jnp.where(real, values, 0.0).astype(BF16), wave


def swap(values, axis):
    return lax.all_to_all(values, axis, 0, 0, tiled=True)


def per_device(field, cotangent, spectral_filter):
    lat = lax.axis_index("lat")
    spacing = 2.0 * math.pi / POINTS
    table, wave = fourier_table()
    doubling = jnp.where(wave == 0, 1.0, 2.0).astype(F32)
    plain = jnp.ones((1, MUDIM), F32)
    theta = ((lat * JLOC + jnp.arange(JPAD)).astype(F32) + 0.5) * (math.pi / (JLOC * LAT))
    quadrature = jnp.broadcast_to(
        (spacing * math.pi / (JLOC * LAT) * jnp.sin(theta))[:, None], (JPAD, 128)
    )
    ones = jnp.ones((JPAD, 128), F32)
    tables = legendre_tables(lat)
    weights = jnp.pad(
        jnp.transpose(spectral_filter.astype(F32), (0, 2, 1)), ((0, 0), (0, 0), (0, LPAD - DEG))
    )
    weights = jnp.broadcast_to(weights[:, :, None, :], (2, CH, TG, LPAD))

    field_shares = swap(to_shares(field), "lon")
    cot_shares = swap(to_shares(cotangent), "lon")
    field_waves = swap(to_waves(field_shares, table, quadrature, plain), "lat")
    cot_waves = swap(to_waves(cot_shares, table, ones, doubling), "lat")

    analysis_spec = pl.BlockSpec((1, 2, CH, TG, LPAD), lambda g: (g, 0, 0, 0, 0))
    out_waves, analysis = spectral_stage(
        forward_kernel,
        tables,
        field_waves,
        weights,
        [],
        (jax.ShapeDtypeStruct((GROUPS, 2, CH, TG, LPAD), F32), analysis_spec),
    )
    grad_waves, terms = spectral_stage(
        backward_kernel,
        tables,
        cot_waves,
        weights,
        [(analysis, analysis_spec)],
        (
            jax.ShapeDtypeStruct((2, CH, TG, LPAD), F32),
            pl.BlockSpec((2, CH, TG, LPAD), lambda g: (0, 0, 0, 0)),
        ),
    )
    output = from_shares(
        swap(from_waves(swap(out_waves, "lat"), table, ones, doubling), "lon")
    )
    grad_field = from_shares(
        swap(from_waves(swap(grad_waves, "lat"), table, quadrature, plain), "lon")
    )
    summed = jnp.sum(terms, axis=2)
    for bit in range(4):
        pairs = [(i, i ^ (1 << bit)) for i in range(LAT)]
        summed = summed + lax.ppermute(summed, "lat", pairs)
    grad_filter = jnp.transpose(summed[:, :, :DEG], (0, 2, 1))
    return (output, grad_field, grad_filter)


def solution(mesh):
    in_specs = (P("lon", "lat", None), P("lon", "lat", None), P(None, None, "lon"))
    out_specs = (P("lon", "lat", None), P("lon", "lat", None), P(None, None, "lon"))
    return jax.shard_map(
        per_device, mesh=mesh, in_specs=in_specs, out_specs=out_specs, check_vma=False
    )
```

```python
import functools
import math

import jax
import jax.numpy as jnp
from jax import lax
from jax.experimental import pallas as pl
from jax.experimental.pallas import tpu as pltpu
from jax.sharding import PartitionSpec as P

LAT, LON = 16, 32
NLOC, JLOC = 45, 45
NPAD, JPAD = 48, 48
CH = 8
NT = NPAD // 16
KDIM = LON * NPAD
MUDIM = 1024
GROUPS, TG = 4, 8
JALL = LAT * JPAD
JHALF = JALL // 2
DEG, LPAD = 720, 768
LHALF = LPAD // 2
POINTS = NLOC * LON
F32, BF16 = jnp.float32, jnp.bfloat16
MIB = 1 << 20


def exchange(tiles, tile_bit, lane_bit):
    step = 1 << lane_bit
    lane = lax.broadcasted_iota(jnp.int32, tiles[0].shape, 1)
    low = (lane & step) == 0
    out = list(tiles)
    for first in range(len(tiles)):
        second = first | (1 << tile_bit)
        if second == first:
            continue
        a, b = tiles[first], tiles[second]
        out[first] = jnp.where(low, a, pltpu.roll(b, step, 1))
        out[second] = jnp.where(low, pltpu.roll(a, 128 - step, 1), b)
    return out


def cost(flops, size):
    return pl.CostEstimate(flops=int(flops), bytes_accessed=int(size), transcendentals=0)


def params(mib):
    return pltpu.CompilerParams(vmem_limit_bytes=mib * MIB)


def share_kernel(x_ref, o_ref):
    def body(nt, jr):
        rows = pl.ds(pl.multiple_of(jr * 16, 16), 16)
        for h in range(2):
            tiles = [
                x_ref[nt * 16 + n, rows, h * 128 : h * 128 + 128].astype(F32) for n in range(16)
            ]
            for b in range(4):
                tiles = exchange(tiles, b, 3 + b)
            for k in range(16):
                o_ref[h * 16 + k, nt, rows, :] = tiles[k].astype(BF16)

    @pl.loop(0, NT * 3, unroll=3)
    def _(s):
        body(s // 3, s % 3)


def to_shares(grid):
    padded = jnp.pad(grid, ((0, NPAD - NLOC), (0, JPAD - JLOC), (0, 0)))
    return pl.pallas_call(
        share_kernel,
        out_shape=jax.ShapeDtypeStruct((LON, NT, JPAD, 128), BF16),
        in_specs=[pl.BlockSpec(memory_space=pltpu.VMEM)],
        out_specs=pl.BlockSpec(memory_space=pltpu.VMEM),
        compiler_params=params(32),
        cost_estimate=cost(1e7, 2.4e6),
        name="to_shares",
    )(padded)


def unshare_kernel(x_ref, o_ref):
    for nt in range(NT):
        for jr in range(3):
            rows = pl.ds(jr * 16, 16)
            count = min(16, JLOC - jr * 16)
            for h in range(2):
                tiles = [x_ref[h * 16 + k, nt, rows, :].astype(F32) for k in range(16)]
                for b in range(4):
                    tiles = exchange(tiles, b, 3 + b)
                for n in range(min(16, NLOC - nt * 16)):
                    o_ref[nt * 16 + n, jr * 16 : jr * 16 + count, h * 128 : h * 128 + 128] = (
                        tiles[n].astype(BF16)[:count]
                    )


def from_shares(shares):
    return pl.pallas_call(
        unshare_kernel,
        out_shape=jax.ShapeDtypeStruct((NLOC, JLOC, 256), BF16),
        in_specs=[pl.BlockSpec(memory_space=pltpu.VMEM)],
        out_specs=pl.BlockSpec(memory_space=pltpu.VMEM),
        compiler_params=params(32),
        cost_estimate=cost(1e7, 2.4e6),
        name="from_shares",
    )(shares)


def fourier_kernel(x_ref, f_ref, row_ref, lane_ref, o_ref, xs_ref, ys_ref):
    @pl.loop(0, 3 * (KDIM // 128), unroll=6)
    def _(s):
        jr, q8 = s // (KDIM // 128), s % (KDIM // 128)
        rows = pl.ds(pl.multiple_of(jr * 16, 16), 16)
        tiles = [x_ref[q8 * 8 + q, rows, :].astype(F32) for q in range(8)]
        for b in range(3):
            tiles = exchange(tiles, b, b)
        lanes = pl.ds(pl.multiple_of(q8 * 128, 128), 128)
        for c in range(8):
            xs_ref[pl.ds(pl.multiple_of(jr * 128 + c * 16, 16), 16), lanes] = tiles[c].astype(BF16)

    ys_ref[...] = jnp.dot(xs_ref[...], f_ref[...], preferred_element_type=F32)

    @pl.loop(0, 3 * 8, unroll=6)
    def _(s):
        jr, ii = s // 8, s % 8
        rows = pl.ds(pl.multiple_of(jr * 16, 16), 16)
        lanes = pl.ds(pl.multiple_of(ii * 128, 128), 128)
        scale = row_ref[rows, :] * lane_ref[:, lanes]
        tiles = [
            ys_ref[pl.ds(pl.multiple_of(jr * 128 + c * 16, 16), 16), lanes] * scale
            for c in range(8)
        ]
        for b in range(3):
            tiles = exchange(tiles, b, 4 + b)
        for i_lo in range(2):
            for g in range(GROUPS):
                o_ref[ii * 2 + i_lo, g, rows, :] = tiles[i_lo * 4 + g].astype(BF16)


def to_waves(shares, table, row_scale, lane_scale):
    return pl.pallas_call(
        fourier_kernel,
        out_shape=jax.ShapeDtypeStruct((LAT, GROUPS, JPAD, 128), BF16),
        in_specs=[pl.BlockSpec(memory_space=pltpu.VMEM)] * 4,
        out_specs=pl.BlockSpec(memory_space=pltpu.VMEM),
        scratch_shapes=[
            pltpu.VMEM((CH * JPAD, KDIM), BF16),
            pltpu.VMEM((CH * JPAD, MUDIM), F32),
        ],
        compiler_params=params(32),
        cost_estimate=cost(2 * 384 * KDIM * MUDIM, 5e6),
        name="to_waves",
    )(shares.reshape(LON * NT, JPAD, 128), table, row_scale, lane_scale)


def inverse_kernel(v_ref, f_ref, row_ref, lane_ref, o_ref, vs_ref, ys_ref):
    @pl.loop(0, 3 * 8, unroll=6)
    def _(s):
        jr, ii = s // 8, s % 8
        rows = pl.ds(pl.multiple_of(jr * 16, 16), 16)
        lanes = pl.ds(pl.multiple_of(ii * 128, 128), 128)
        tiles = [
            v_ref[ii * 2 + i_lo, g, rows, :].astype(F32) for i_lo in range(2) for g in range(GROUPS)
        ]
        for b in range(3):
            tiles = exchange(tiles, b, 4 + b)
        scale = lane_ref[:, lanes]
        for c in range(8):
            vs_ref[pl.ds(pl.multiple_of(jr * 128 + c * 16, 16), 16), lanes] = (
                tiles[c] * scale
            ).astype(BF16)

    ys_ref[...] = lax.dot_general(
        vs_ref[...], f_ref[...], (((1,), (1,)), ((), ())), preferred_element_type=F32
    )

    @pl.loop(0, 3 * (KDIM // 128), unroll=6)
    def _(s):
        jr, q8 = s // (KDIM // 128), s % (KDIM // 128)
        rows = pl.ds(pl.multiple_of(jr * 16, 16), 16)
        lanes = pl.ds(pl.multiple_of(q8 * 128, 128), 128)
        scale = row_ref[rows, :]
        tiles = [
            ys_ref[pl.ds(pl.multiple_of(jr * 128 + c * 16, 16), 16), lanes] * scale
            for c in range(8)
        ]
        for b in range(3):
            tiles = exchange(tiles, b, b)
        for q in range(8):
            o_ref[q8 * 8 + q, rows, :] = tiles[q].astype(BF16)


def from_waves(waves, table, row_scale, lane_scale):
    return pl.pallas_call(
        inverse_kernel,
        out_shape=jax.ShapeDtypeStruct((LON * NT, JPAD, 128), BF16),
        in_specs=[pl.BlockSpec(memory_space=pltpu.VMEM)] * 4,
        out_specs=pl.BlockSpec(memory_space=pltpu.VMEM),
        scratch_shapes=[
            pltpu.VMEM((CH * JPAD, MUDIM), BF16),
            pltpu.VMEM((CH * JPAD, KDIM), F32),
        ],
        compiler_params=params(32),
        cost_estimate=cost(2 * 384 * KDIM * MUDIM, 5e6),
        name="from_waves",
    )(waves, table, row_scale, lane_scale).reshape(LON, NT, JPAD, 128)


LCHUNK = 128


def legendre_kernel(m_ref, f_ref, h_ref, x_ref, p0_ref, e0_ref, o_ref, p1_s, p2_s, e_s, rows_s):
    g, lc = pl.program_id(0), pl.program_id(1)

    @pl.when(lc == 0)
    def _():
        p1_s[...] = jnp.zeros_like(p1_s)
        p2_s[...] = jnp.zeros_like(p2_s)
        e_s[...] = e0_ref[0]

    @pl.when(lc < g)
    def _():
        o_ref[...] = jnp.zeros_like(o_ref)

    def chunk(starts):
        x = jnp.broadcast_to(x_ref[...], (TG, JHALF))
        orders = jnp.broadcast_to(m_ref[0][:, :1], (TG, JHALF))
        p1, p2, e = p1_s[...], p2_s[...], e_s[...]
        for u in range(LCHUNK):
            if u % 8 == 0:
                big = jnp.abs(p1) > 2.0**24
                down = jnp.where(big, 2.0**-48, 1.0)
                p1, p2 = p1 * down, p2 * down
                e = jnp.where(big, e + 48.0, e)
                scale = jnp.exp2(jnp.maximum(e, -200.0))
            new = (f_ref[0][:, u : u + 1] * x) * p1 - h_ref[0][:, u : u + 1] * p2
            if starts:
                degree = (lc * LCHUNK + u).astype(F32)
                new = jnp.where(orders == degree, p0_ref[0], new)
            p1, p2 = new, p1
            value = new * scale
            for b in range(JHALF // 128):
                rows_s[b, u * TG : u * TG + TG, :] = value[:, b * 128 : b * 128 + 128]
        p1_s[...] = p1
        p2_s[...] = p2
        e_s[...] = e
        for t in range(TG):
            for odd in range(2):
                for b in range(JHALF // 128):
                    o_ref[t, odd, :, b * 128 : b * 128 + 128] = rows_s[
                        b, pl.ds(odd * TG + t, LCHUNK // 2, stride=2 * TG), :
                    ].astype(BF16)

    pl.when(lc == g)(functools.partial(chunk, True))
    pl.when(lc > g)(functools.partial(chunk, False))


def legendre_tables(lat):
    order = (lat + LAT * jnp.arange(GROUPS * TG, dtype=jnp.int32)).astype(F32)[:, None]
    degrees = jnp.arange(LPAD, dtype=F32)[None, :]

    def factor_at(degree):
        inside = degree > order
        top = jnp.where(inside, 4.0 * degree * degree - 1.0, 1.0)
        low = jnp.where(inside, degree * degree - order * order, 1.0)
        return jnp.sqrt(top / low), inside

    factor, inside = factor_at(degrees)
    earlier, earlier_inside = factor_at(degrees - 1.0)
    forward = jnp.where(inside, factor, 0.0).reshape(GROUPS, TG, LPAD)
    back = jnp.where(earlier_inside, factor / earlier, 0.0).reshape(GROUPS, TG, LPAD)
    start_log = 0.5 * (
        lax.lgamma(order + 1.5) - lax.lgamma(jnp.float32(1.5)) - lax.lgamma(order + 1.0)
    ) - 0.5 * math.log(4.0 * math.pi)
    place = jnp.arange(JHALF, dtype=jnp.int32)
    cycle = place // JPAD * JLOC + jnp.minimum(place % JPAD, JLOC - 1)
    theta = (cycle.astype(F32) + 0.5) * (math.pi / (JLOC * LAT))
    start = (start_log + order * jnp.log(jnp.sin(theta))[None, :]) * (1.0 / math.log(2.0))
    exponent = jnp.floor(start)
    real = (place % JPAD < JLOC)[None, :]
    mantissa = jnp.where(real, jnp.exp2(start - exponent), 0.0)
    orders = jnp.broadcast_to(order, (GROUPS * TG, 128)).reshape(GROUPS, TG, 128)
    return pl.pallas_call(
        legendre_kernel,
        grid=(GROUPS, LPAD // LCHUNK),
        out_shape=jax.ShapeDtypeStruct((GROUPS * TG, 2, LHALF, JHALF), BF16),
        in_specs=[
            pl.BlockSpec((1, TG, 128), lambda g, lc: (g, 0, 0)),
            pl.BlockSpec((1, TG, LCHUNK), lambda g, lc: (g, 0, lc)),
            pl.BlockSpec((1, TG, LCHUNK), lambda g, lc: (g, 0, lc)),
            pl.BlockSpec((1, JHALF), lambda g, lc: (0, 0)),
            pl.BlockSpec((1, TG, JHALF), lambda g, lc: (g, 0, 0)),
            pl.BlockSpec((1, TG, JHALF), lambda g, lc: (g, 0, 0)),
        ],
        out_specs=pl.BlockSpec((TG, 2, LCHUNK // 2, JHALF), lambda g, lc: (g, 0, lc, 0)),
        scratch_shapes=[pltpu.VMEM((TG, JHALF), F32)] * 3
        + [pltpu.VMEM((JHALF // 128, LCHUNK * TG, 128), F32)],
        compiler_params=params(32),
        cost_estimate=cost(2.5e10, 2e7),
        name="legendre_tables",
    )(
        orders,
        forward,
        back,
        jnp.cos(theta)[None, :],
        mantissa.reshape(GROUPS, TG, JHALF),
        exponent.reshape(GROUPS, TG, JHALF),
    )


def spectral_body(p_ref, z_ref, w_ref, fold_ref, sign, o_ref, s_ref, k_ref, u_ref):
    lane = lax.broadcasted_iota(jnp.int32, (JHALF, 128), 1) % TG
    row = lax.broadcasted_iota(jnp.int32, (128, LHALF), 0) % TG
    z = z_ref[:, 0].reshape(JALL, 128)
    folded = jnp.dot(fold_ref[...], z, preferred_element_type=F32)

    def products(g):
        first = 64 * g
        for odd in range(2):
            half = folded[odd * JHALF : odd * JHALF + JHALF]
            total = None
            for t in range(TG):
                part = jnp.dot(
                    p_ref[t, odd, first:, :],
                    jnp.where(lane == t, half, 0.0).astype(BF16),
                    preferred_element_type=F32,
                )
                total = part if t == 0 else total + part
            if first:
                s_ref[odd * LHALF : odd * LHALF + first, :] = jnp.zeros((first, 128), F32)
            s_ref[odd * LHALF + first : odd * LHALF + LHALF, :] = total

    def back_products(g):
        first = g // 2 * 128
        for odd in range(2):
            half = k_ref[:, odd * LHALF + first : odd * LHALF + LHALF]
            total = None
            for t in range(TG):
                part = jnp.dot(
                    jnp.where(row[:, first:] == t, half, 0.0).astype(BF16),
                    p_ref[t, odd, first:, :],
                    preferred_element_type=F32,
                )
                total = part if t == 0 else total + part
            u_ref[:, odd * JHALF : odd * JHALF + JHALF] = total.astype(BF16)

    for g in range(GROUPS):
        pl.when(pl.program_id(0) == g)(functools.partial(products, g))
    found = s_ref[...].T.reshape(CH, 2, TG, LPAD)
    real, imag = found[:, 0], found[:, 1]
    cross = w_ref[1] * sign
    kept = jnp.stack([w_ref[0] * real - cross * imag, w_ref[0] * imag + cross * real], axis=1)
    k_ref[...] = kept.reshape(128, LPAD)
    for g in range(GROUPS):
        pl.when(pl.program_id(0) == g)(functools.partial(back_products, g))
    spread = jnp.dot(u_ref[...], fold_ref[...], preferred_element_type=F32)
    o_ref[:, 0] = spread.T.astype(BF16).reshape(LAT, JPAD, 128)
    return real, imag


def forward_kernel(p_ref, z_ref, w_ref, fold_ref, o_ref, a_ref, *scratch):
    real, imag = spectral_body(p_ref, z_ref, w_ref, fold_ref, 1.0, o_ref, *scratch)
    a_ref[0, 0] = real
    a_ref[0, 1] = imag


def backward_kernel(p_ref, z_ref, w_ref, fold_ref, a_ref, o_ref, g_ref, *scratch):
    real, imag = spectral_body(p_ref, z_ref, w_ref, fold_ref, -1.0, o_ref, *scratch)
    first, second = a_ref[0, 0], a_ref[0, 1]

    @pl.when(pl.program_id(0) == 0)
    def _():
        g_ref[...] = jnp.zeros_like(g_ref)

    g_ref[0] += first * real + second * imag
    g_ref[1] += first * imag - second * real


def spectral_stage(kernel, tables, spectra, weights, fold, extra_in, extra_out):
    wave_spec = pl.BlockSpec((LAT, 1, JPAD, 128), lambda g: (0, g, 0, 0))
    return pl.pallas_call(
        kernel,
        grid=(GROUPS,),
        out_shape=(jax.ShapeDtypeStruct((LAT, GROUPS, JPAD, 128), BF16), extra_out[0]),
        in_specs=[
            pl.BlockSpec((TG, 2, LHALF, JHALF), lambda g: (g, 0, 0, 0)),
            wave_spec,
            pl.BlockSpec((2, CH, TG, LPAD), lambda g: (0, 0, 0, 0)),
            pl.BlockSpec((JALL, JALL), lambda g: (0, 0)),
        ]
        + [spec for _, spec in extra_in],
        out_specs=(wave_spec, extra_out[1]),
        scratch_shapes=[
            pltpu.VMEM((LPAD, 128), F32),
            pltpu.VMEM((128, LPAD), F32),
            pltpu.VMEM((128, JALL), BF16),
        ],
        compiler_params=params(48),
        cost_estimate=cost(1.2e10, 2.2e7),
        name="spectral_stage",
    )(tables, spectra, weights, fold, *[value for value, _ in extra_in])


def table_kernel(c1_ref, s1_ref, c2_ref, s2_ref, o_ref):
    @pl.loop(0, MUDIM // 128)
    def _(lc):
        lanes = pl.ds(pl.multiple_of(lc * 128, 128), 128)
        row = lax.broadcasted_iota(jnp.int32, (8, 128), 0)
        for start in range(NT):
            part = (row + 2 * start) % NT
            for pair in range(8):
                picked = []
                for n in (2 * pair, 2 * pair + 1):
                    for ref in (c2_ref, s2_ref):
                        rows = [
                            jnp.broadcast_to(ref[nt * 16 + n : nt * 16 + n + 1, lanes], (8, 128))
                            for nt in range(NT)
                        ]
                        picked.append(
                            jnp.where(part == 0, rows[0], jnp.where(part == 1, rows[1], rows[2]))
                        )
                for block in range(start, KDIM // 128, NT):
                    c1 = c1_ref[block * 8 : block * 8 + 8, lanes]
                    s1 = s1_ref[block * 8 : block * 8 + 8, lanes]
                    o_ref[block * 128 + pair * 16 : block * 128 + pair * 16 + 16, lanes] = (
                        jnp.concatenate(
                            [c1 * picked[0] - s1 * picked[1], c1 * picked[2] - s1 * picked[3]],
                            axis=0,
                        ).astype(BF16)
                    )


def fourier_table():
    mu = jnp.arange(MUDIM, dtype=jnp.int32)
    lat = mu // 128 * 2 + mu // 64 % 2
    wave = (lat + LAT * (mu // 16 % 4 * TG + mu % TG))[None, :]
    quarter = (mu // 8 % 2 * (POINTS // 4))[None, :]
    origin = (jnp.arange(LON * NT, dtype=jnp.int32) // NT * NLOC)[:, None]
    local = jnp.arange(NPAD, dtype=jnp.int32)[:, None]
    first = ((wave * origin + quarter) % POINTS).astype(F32) * (2.0 * math.pi / POINTS)
    second = (wave * local % POINTS).astype(F32) * (2.0 * math.pi / POINTS)
    table = pl.pallas_call(
        table_kernel,
        out_shape=jax.ShapeDtypeStruct((KDIM, MUDIM), BF16),
        in_specs=[pl.BlockSpec(memory_space=pltpu.VMEM)] * 4,
        out_specs=pl.BlockSpec(memory_space=pltpu.VMEM),
        compiler_params=params(32),
        cost_estimate=cost(1e7, 4e6),
        name="fourier_table",
    )(
        jnp.cos(first),
        jnp.sin(first),
        jnp.where(local < NLOC, jnp.cos(second), 0.0),
        jnp.where(local < NLOC, jnp.sin(second), 0.0),
    )
    return table, wave


def fold_matrix(lat):
    row = jnp.arange(JALL, dtype=jnp.int32)[:, None]
    column = jnp.arange(JALL, dtype=jnp.int32)[None, :]
    odd, band, place = row // JHALF, row % JHALF // JPAD, row % JPAD
    sign = jnp.where((odd + lat) % 2 == 0, 1.0, -1.0)
    same = (row % JHALF == column) & (place < JLOC)
    mirror = (column // JPAD == LAT - 1 - band) & (column % JPAD == JLOC - 1 - place)
    return jnp.where(same, 1.0, jnp.where(mirror, sign, 0.0)).astype(BF16)


def swap(values, axis):
    return lax.all_to_all(values, axis, 0, 0, tiled=True)


def per_device(field, cotangent, spectral_filter):
    lat = lax.axis_index("lat")
    spacing = 2.0 * math.pi / POINTS
    table, wave = fourier_table()
    doubling = jnp.where(wave == 0, 1.0, 2.0).astype(F32)
    plain = jnp.ones((1, MUDIM), F32)
    theta = ((lat * JLOC + jnp.arange(JPAD)).astype(F32) + 0.5) * (math.pi / (JLOC * LAT))
    quadrature = jnp.broadcast_to(
        (spacing * math.pi / (JLOC * LAT) * jnp.sin(theta))[:, None], (JPAD, 128)
    )
    ones = jnp.ones((JPAD, 128), F32)
    tables = legendre_tables(lat)
    weights = jnp.transpose(
        spectral_filter.astype(F32).reshape(2, DEG // 2, 2, CH), (0, 3, 2, 1)
    )
    weights = jnp.pad(weights, ((0, 0), (0, 0), (0, 0), (0, (LPAD - DEG) // 2)))
    weights = weights.reshape(2, CH, LPAD)
    fold = fold_matrix(lat)
    weights = jnp.broadcast_to(weights[:, :, None, :], (2, CH, TG, LPAD))

    field_shares = swap(to_shares(field), "lon")
    cot_local, table, tables = lax.optimization_barrier((to_shares(cotangent), table, tables))
    cot_shares = swap(cot_local, "lon")
    field_waves = swap(to_waves(field_shares, table, quadrature, plain), "lat")
    cot_waves = swap(to_waves(cot_shares, table, ones, doubling), "lat")

    analysis_spec = pl.BlockSpec((1, 2, CH, TG, LPAD), lambda g: (g, 0, 0, 0, 0))
    out_waves, analysis = spectral_stage(
        forward_kernel,
        tables,
        field_waves,
        weights,
        fold,
        [],
        (jax.ShapeDtypeStruct((GROUPS, 2, CH, TG, LPAD), F32), analysis_spec),
    )
    grad_waves, terms = spectral_stage(
        backward_kernel,
        tables,
        cot_waves,
        weights,
        fold,
        [(analysis, analysis_spec)],
        (
            jax.ShapeDtypeStruct((2, CH, TG, LPAD), F32),
            pl.BlockSpec((2, CH, TG, LPAD), lambda g: (0, 0, 0, 0)),
        ),
    )
    output = from_shares(
        swap(from_waves(swap(out_waves, "lat"), table, ones, doubling), "lon")
    )
    grad_field = from_shares(
        swap(from_waves(swap(grad_waves, "lat"), table, quadrature, plain), "lon")
    )
    summed = jnp.sum(terms, axis=2)
    for bit in range(4):
        pairs = [(i, i ^ (1 << bit)) for i in range(LAT)]
        summed = summed + lax.ppermute(summed, "lat", pairs)
    summed = summed.reshape(2, CH, 2, LHALF)[:, :, :, : DEG // 2]
    grad_filter = jnp.transpose(summed, (0, 3, 2, 1)).reshape(2, DEG, CH)
    return (output, grad_field, grad_filter)


def solution(mesh):
    in_specs = (P("lon", "lat", None), P("lon", "lat", None), P(None, None, "lon"))
    out_specs = (P("lon", "lat", None), P("lon", "lat", None), P(None, None, "lon"))
    return jax.shard_map(
        per_device, mesh=mesh, in_specs=in_specs, out_specs=out_specs, check_vma=False
    )
```

```python
import functools
import math

import jax
import jax.numpy as jnp
from jax import lax
from jax.experimental import pallas as pl
from jax.experimental.pallas import tpu as pltpu
from jax.sharding import PartitionSpec as P

LAT, LON = 16, 32
NLOC, JLOC = 45, 45
NPAD, JPAD = 48, 48
CH = 8
NT = NPAD // 16
KDIM = LON * NPAD
MUDIM = 1024
GROUPS, TG = 4, 8
JALL = LAT * JPAD
JHALF = JALL // 2
DEG, LPAD = 720, 768
LHALF = LPAD // 2
POINTS = NLOC * LON
F32, BF16 = jnp.float32, jnp.bfloat16
MIB = 1 << 20


def exchange(tiles, tile_bit, lane_bit):
    step = 1 << lane_bit
    lane = lax.broadcasted_iota(jnp.int32, tiles[0].shape, 1)
    low = (lane & step) == 0
    out = list(tiles)
    for first in range(len(tiles)):
        second = first | (1 << tile_bit)
        if second == first:
            continue
        a, b = tiles[first], tiles[second]
        out[first] = jnp.where(low, a, pltpu.roll(b, step, 1))
        out[second] = jnp.where(low, pltpu.roll(a, 128 - step, 1), b)
    return out


def cost(flops, size):
    return pl.CostEstimate(flops=int(flops), bytes_accessed=int(size), transcendentals=0)


def params(mib):
    return pltpu.CompilerParams(vmem_limit_bytes=mib * MIB)


def share_kernel(x_ref, o_ref):
    for nt in range(NT):
        for jr in range(3):
            rows = slice(jr * 16, jr * 16 + 16)
            count = min(16, JLOC - jr * 16)
            for h in range(2):
                lanes = slice(h * 128, h * 128 + 128)
                tiles = []
                for n in range(nt * 16, nt * 16 + 16):
                    if n >= NLOC:
                        tiles.append(jnp.zeros((16, 128), F32))
                        continue
                    tile = x_ref[n, jr * 16 : jr * 16 + count, lanes].astype(F32)
                    if count < 16:
                        tile = jnp.concatenate([tile, jnp.zeros((16 - count, 128), F32)], axis=0)
                    tiles.append(tile)
                for b in range(4):
                    tiles = exchange(tiles, b, 3 + b)
                for k in range(16):
                    o_ref[h * 16 + k, nt, rows, :] = tiles[k].astype(BF16)


def to_shares(grid):
    return pl.pallas_call(
        share_kernel,
        out_shape=pltpu.HBM((LON, NT, JPAD, 128), BF16),
        compiler_params=params(32),
        cost_estimate=cost(1e7, 2.4e6),
        name="to_shares",
    )(grid)


def unshare_kernel(x_ref, o_ref):
    for nt in range(NT):
        for jr in range(3):
            rows = pl.ds(jr * 16, 16)
            count = min(16, JLOC - jr * 16)
            for h in range(2):
                tiles = [x_ref[h * 16 + k, nt, rows, :].astype(F32) for k in range(16)]
                for b in range(4):
                    tiles = exchange(tiles, b, 3 + b)
                for n in range(min(16, NLOC - nt * 16)):
                    o_ref[nt * 16 + n, jr * 16 : jr * 16 + count, h * 128 : h * 128 + 128] = (
                        tiles[n].astype(BF16)[:count]
                    )


def from_shares(shares):
    return pl.pallas_call(
        unshare_kernel,
        out_shape=jax.ShapeDtypeStruct((NLOC, JLOC, 256), BF16),
        in_specs=[pl.BlockSpec(memory_space=pltpu.VMEM)],
        out_specs=pl.BlockSpec(memory_space=pltpu.VMEM),
        compiler_params=params(32),
        cost_estimate=cost(1e7, 2.4e6),
        name="from_shares",
    )(shares)


def fourier_kernel(x_ref, f_ref, row_ref, lane_ref, o_ref, xs_ref, ys_ref):
    @pl.loop(0, 3 * (KDIM // 128), unroll=6)
    def _(s):
        jr, q8 = s // (KDIM // 128), s % (KDIM // 128)
        rows = pl.ds(pl.multiple_of(jr * 16, 16), 16)
        tiles = [x_ref[q8 * 8 + q, rows, :].astype(F32) for q in range(8)]
        for b in range(3):
            tiles = exchange(tiles, b, b)
        lanes = pl.ds(pl.multiple_of(q8 * 128, 128), 128)
        for c in range(8):
            xs_ref[pl.ds(pl.multiple_of(jr * 128 + c * 16, 16), 16), lanes] = tiles[c].astype(BF16)

    ys_ref[...] = jnp.dot(xs_ref[...], f_ref[...], preferred_element_type=F32)

    @pl.loop(0, 3 * 8, unroll=6)
    def _(s):
        jr, ii = s // 8, s % 8
        rows = pl.ds(pl.multiple_of(jr * 16, 16), 16)
        lanes = pl.ds(pl.multiple_of(ii * 128, 128), 128)
        scale = row_ref[rows, :] * lane_ref[:, lanes]
        tiles = [
            ys_ref[pl.ds(pl.multiple_of(jr * 128 + c * 16, 16), 16), lanes] * scale
            for c in range(8)
        ]
        for b in range(3):
            tiles = exchange(tiles, b, 4 + b)
        for i_lo in range(2):
            for g in range(GROUPS):
                o_ref[ii * 2 + i_lo, g, rows, :] = tiles[i_lo * 4 + g].astype(BF16)


def to_waves(shares, table, row_scale, lane_scale):
    return pl.pallas_call(
        fourier_kernel,
        out_shape=pltpu.HBM((LAT, GROUPS, JPAD, 128), BF16),
        in_specs=[pl.BlockSpec(memory_space=pltpu.VMEM)] * 4,
        scratch_shapes=[
            pltpu.VMEM((CH * JPAD, KDIM), BF16),
            pltpu.VMEM((CH * JPAD, MUDIM), F32),
        ],
        compiler_params=params(32),
        cost_estimate=cost(2 * 384 * KDIM * MUDIM, 5e6),
        name="to_waves",
    )(shares.reshape(LON * NT, JPAD, 128), table, row_scale, lane_scale)


def inverse_kernel(v_ref, f_ref, row_ref, lane_ref, o_ref, vs_ref, ys_ref):
    @pl.loop(0, 3 * 8, unroll=6)
    def _(s):
        jr, ii = s // 8, s % 8
        rows = pl.ds(pl.multiple_of(jr * 16, 16), 16)
        lanes = pl.ds(pl.multiple_of(ii * 128, 128), 128)
        tiles = [
            v_ref[ii * 2 + i_lo, g, rows, :].astype(F32) for i_lo in range(2) for g in range(GROUPS)
        ]
        for b in range(3):
            tiles = exchange(tiles, b, 4 + b)
        scale = lane_ref[:, lanes]
        for c in range(8):
            vs_ref[pl.ds(pl.multiple_of(jr * 128 + c * 16, 16), 16), lanes] = (
                tiles[c] * scale
            ).astype(BF16)

    ys_ref[...] = lax.dot_general(
        vs_ref[...], f_ref[...], (((1,), (1,)), ((), ())), preferred_element_type=F32
    )

    @pl.loop(0, 3 * (KDIM // 128), unroll=6)
    def _(s):
        jr, q8 = s // (KDIM // 128), s % (KDIM // 128)
        rows = pl.ds(pl.multiple_of(jr * 16, 16), 16)
        lanes = pl.ds(pl.multiple_of(q8 * 128, 128), 128)
        scale = row_ref[rows, :]
        tiles = [
            ys_ref[pl.ds(pl.multiple_of(jr * 128 + c * 16, 16), 16), lanes] * scale
            for c in range(8)
        ]
        for b in range(3):
            tiles = exchange(tiles, b, b)
        for q in range(8):
            o_ref[q8 * 8 + q, rows, :] = tiles[q].astype(BF16)


def from_waves(waves, table, row_scale, lane_scale):
    return pl.pallas_call(
        inverse_kernel,
        out_shape=pltpu.HBM((LON * NT, JPAD, 128), BF16),
        in_specs=[pl.BlockSpec(memory_space=pltpu.VMEM)] * 4,
        scratch_shapes=[
            pltpu.VMEM((CH * JPAD, MUDIM), BF16),
            pltpu.VMEM((CH * JPAD, KDIM), F32),
        ],
        compiler_params=params(32),
        cost_estimate=cost(2 * 384 * KDIM * MUDIM, 5e6),
        name="from_waves",
    )(waves, table, row_scale, lane_scale).reshape(LON, NT, JPAD, 128)


LCHUNK = 128


def legendre_kernel(m_ref, f_ref, h_ref, x_ref, p0_ref, e0_ref, o_ref, p1_s, p2_s, e_s, rows_s):
    g, lc = pl.program_id(0), pl.program_id(1)

    @pl.when(lc == 0)
    def _():
        p1_s[...] = jnp.zeros_like(p1_s)
        p2_s[...] = jnp.zeros_like(p2_s)
        e_s[...] = e0_ref[0]

    @pl.when(lc < g)
    def _():
        o_ref[...] = jnp.zeros_like(o_ref)

    def chunk(starts):
        x = jnp.broadcast_to(x_ref[...], (TG, JHALF))
        orders = jnp.broadcast_to(m_ref[0][:, :1], (TG, JHALF))
        p1, p2, e = p1_s[...], p2_s[...], e_s[...]
        for u in range(LCHUNK):
            if u % 8 == 0:
                big = jnp.abs(p1) > 2.0**24
                down = jnp.where(big, 2.0**-48, 1.0)
                p1, p2 = p1 * down, p2 * down
                e = jnp.where(big, e + 48.0, e)
                scale = jnp.exp2(jnp.maximum(e, -200.0))
            new = (f_ref[0][:, u : u + 1] * x) * p1 - h_ref[0][:, u : u + 1] * p2
            if starts:
                degree = (lc * LCHUNK + u).astype(F32)
                new = jnp.where(orders == degree, p0_ref[0], new)
            p1, p2 = new, p1
            value = new * scale
            for b in range(JHALF // 128):
                rows_s[b, u * TG : u * TG + TG, :] = value[:, b * 128 : b * 128 + 128]
        p1_s[...] = p1
        p2_s[...] = p2
        e_s[...] = e
        for t in range(TG):
            for odd in range(2):
                for b in range(JHALF // 128):
                    o_ref[t, odd, :, b * 128 : b * 128 + 128] = rows_s[
                        b, pl.ds(odd * TG + t, LCHUNK // 2, stride=2 * TG), :
                    ].astype(BF16)

    pl.when(lc == g)(functools.partial(chunk, True))
    pl.when(lc > g)(functools.partial(chunk, False))


def legendre_tables(lat):
    order = (lat + LAT * jnp.arange(GROUPS * TG, dtype=jnp.int32)).astype(F32)[:, None]
    degrees = jnp.arange(LPAD, dtype=F32)[None, :]

    def factor_at(degree):
        inside = degree > order
        top = jnp.where(inside, 4.0 * degree * degree - 1.0, 1.0)
        low = jnp.where(inside, degree * degree - order * order, 1.0)
        return jnp.sqrt(top / low), inside

    factor, inside = factor_at(degrees)
    earlier, earlier_inside = factor_at(degrees - 1.0)
    forward = jnp.where(inside, factor, 0.0).reshape(GROUPS, TG, LPAD)
    back = jnp.where(earlier_inside, factor / earlier, 0.0).reshape(GROUPS, TG, LPAD)
    start_log = 0.5 * (
        lax.lgamma(order + 1.5) - lax.lgamma(jnp.float32(1.5)) - lax.lgamma(order + 1.0)
    ) - 0.5 * math.log(4.0 * math.pi)
    place = jnp.arange(JHALF, dtype=jnp.int32)
    cycle = place // JPAD * JLOC + jnp.minimum(place % JPAD, JLOC - 1)
    theta = (cycle.astype(F32) + 0.5) * (math.pi / (JLOC * LAT))
    start = (start_log + order * jnp.log(jnp.sin(theta))[None, :]) * (1.0 / math.log(2.0))
    exponent = jnp.floor(start)
    real = (place % JPAD < JLOC)[None, :]
    mantissa = jnp.where(real, jnp.exp2(start - exponent), 0.0)
    orders = jnp.broadcast_to(order, (GROUPS * TG, 128)).reshape(GROUPS, TG, 128)
    return pl.pallas_call(
        legendre_kernel,
        grid=(GROUPS, LPAD // LCHUNK),
        out_shape=pltpu.HBM((GROUPS * TG, 2, LHALF, JHALF), BF16),
        in_specs=[
            pl.BlockSpec((1, TG, 128), lambda g, lc: (g, 0, 0)),
            pl.BlockSpec((1, TG, LCHUNK), lambda g, lc: (g, 0, lc)),
            pl.BlockSpec((1, TG, LCHUNK), lambda g, lc: (g, 0, lc)),
            pl.BlockSpec((1, JHALF), lambda g, lc: (0, 0)),
            pl.BlockSpec((1, TG, JHALF), lambda g, lc: (g, 0, 0)),
            pl.BlockSpec((1, TG, JHALF), lambda g, lc: (g, 0, 0)),
        ],
        out_specs=pl.BlockSpec((TG, 2, LCHUNK // 2, JHALF), lambda g, lc: (g, 0, lc, 0)),
        scratch_shapes=[pltpu.VMEM((TG, JHALF), F32)] * 3
        + [pltpu.VMEM((JHALF // 128, LCHUNK * TG, 128), F32)],
        compiler_params=params(32),
        cost_estimate=cost(2.5e10, 2e7),
        name="legendre_tables",
    )(
        orders,
        forward,
        back,
        jnp.cos(theta)[None, :],
        mantissa.reshape(GROUPS, TG, JHALF),
        exponent.reshape(GROUPS, TG, JHALF),
    )


def spectral_body(p_ref, z_ref, w_ref, fold_ref, sign, o_ref, s_ref, k_ref, u_ref):
    lane = lax.broadcasted_iota(jnp.int32, (JHALF, 128), 1) % TG
    row = lax.broadcasted_iota(jnp.int32, (128, LHALF), 0) % TG
    z = z_ref[:, 0].reshape(JALL, 128)
    folded = jnp.dot(fold_ref[...], z, preferred_element_type=F32)

    def products(g):
        first = 64 * g
        for odd in range(2):
            half = folded[odd * JHALF : odd * JHALF + JHALF]
            total = None
            for t in range(TG):
                part = jnp.dot(
                    p_ref[t, odd, first:, :],
                    jnp.where(lane == t, half, 0.0).astype(BF16),
                    preferred_element_type=F32,
                )
                total = part if t == 0 else total + part
            if first:
                s_ref[odd * LHALF : odd * LHALF + first, :] = jnp.zeros((first, 128), F32)
            s_ref[odd * LHALF + first : odd * LHALF + LHALF, :] = total

    def back_products(g):
        first = g // 2 * 128
        for odd in range(2):
            half = k_ref[:, odd * LHALF + first : odd * LHALF + LHALF]
            total = None
            for t in range(TG):
                part = jnp.dot(
                    jnp.where(row[:, first:] == t, half, 0.0).astype(BF16),
                    p_ref[t, odd, first:, :],
                    preferred_element_type=F32,
                )
                total = part if t == 0 else total + part
            u_ref[:, odd * JHALF : odd * JHALF + JHALF] = total.astype(BF16)

    for g in range(GROUPS):
        pl.when(pl.program_id(0) == g)(functools.partial(products, g))
    found = s_ref[...].T.reshape(CH, 2, TG, LPAD)
    real, imag = found[:, 0], found[:, 1]
    cross = w_ref[1] * sign
    kept = jnp.stack([w_ref[0] * real - cross * imag, w_ref[0] * imag + cross * real], axis=1)
    k_ref[...] = kept.reshape(128, LPAD)
    for g in range(GROUPS):
        pl.when(pl.program_id(0) == g)(functools.partial(back_products, g))
    spread = jnp.dot(u_ref[...], fold_ref[...], preferred_element_type=F32)
    o_ref[:, 0] = spread.T.astype(BF16).reshape(LAT, JPAD, 128)
    return real, imag


def forward_kernel(p_ref, z_ref, w_ref, fold_ref, o_ref, a_ref, *scratch):
    real, imag = spectral_body(p_ref, z_ref, w_ref, fold_ref, 1.0, o_ref, *scratch)
    a_ref[0, 0] = real
    a_ref[0, 1] = imag


def backward_kernel(p_ref, z_ref, w_ref, fold_ref, a_ref, o_ref, g_ref, *scratch):
    step = pl.program_id(0)

    @pl.when(step == 0)
    def _():
        g_ref[...] = jnp.zeros_like(g_ref)

    @pl.when(step < GROUPS)
    def _():
        real, imag = spectral_body(p_ref, z_ref, w_ref, fold_ref, -1.0, o_ref, *scratch)
        first, second = a_ref[0, 0], a_ref[0, 1]
        g_ref[0] += first * real + second * imag
        g_ref[1] += first * imag - second * real

    for part in range(2):

        @pl.when(step == GROUPS + part)
        def _():
            total = jnp.sum(g_ref[part], axis=1)
            rows = [total[:, b * 128 : b * 128 + 128] for b in range(LPAD // 128)]
            o_ref[:, 0] = jnp.broadcast_to(
                jnp.concatenate(rows, axis=0).astype(BF16)[None], (LAT, JPAD, 128)
            )


def spectral_stage(kernel, steps, tables, spectra, weights, fold, extra_in, extra_out, extra_scratch):
    last = GROUPS - 1
    return pl.pallas_call(
        kernel,
        grid=(steps,),
        out_shape=[pltpu.HBM((LAT, steps, JPAD, 128), BF16)] + [value for value, _ in extra_out],
        in_specs=[
            pl.BlockSpec((TG, 2, LHALF, JHALF), lambda g: (jnp.minimum(g, last), 0, 0, 0)),
            pl.BlockSpec((LAT, 1, JPAD, 128), lambda g: (0, jnp.minimum(g, last), 0, 0)),
            pl.BlockSpec((2, CH, TG, LPAD), lambda g: (0, 0, 0, 0)),
            pl.BlockSpec((JALL, JALL), lambda g: (0, 0)),
        ]
        + [spec for _, spec in extra_in],
        out_specs=[pl.BlockSpec((LAT, 1, JPAD, 128), lambda g: (0, g, 0, 0))]
        + [spec for _, spec in extra_out],
        scratch_shapes=extra_scratch
        + [
            pltpu.VMEM((LPAD, 128), F32),
            pltpu.VMEM((128, LPAD), F32),
            pltpu.VMEM((128, JALL), BF16),
        ],
        compiler_params=params(48),
        cost_estimate=cost(1.2e10, 2.2e7),
        name="spectral_stage",
    )(tables, spectra, weights, fold, *[value for value, _ in extra_in])


def table_kernel(c1_ref, s1_ref, c2_ref, s2_ref, o_ref):
    @pl.loop(0, MUDIM // 128)
    def _(lc):
        lanes = pl.ds(pl.multiple_of(lc * 128, 128), 128)
        row = lax.broadcasted_iota(jnp.int32, (8, 128), 0)
        for start in range(NT):
            part = (row + 2 * start) % NT
            for pair in range(8):
                picked = []
                for n in (2 * pair, 2 * pair + 1):
                    for ref in (c2_ref, s2_ref):
                        rows = [
                            jnp.broadcast_to(ref[nt * 16 + n : nt * 16 + n + 1, lanes], (8, 128))
                            for nt in range(NT)
                        ]
                        picked.append(
                            jnp.where(part == 0, rows[0], jnp.where(part == 1, rows[1], rows[2]))
                        )
                for block in range(start, KDIM // 128, NT):
                    c1 = c1_ref[block * 8 : block * 8 + 8, lanes]
                    s1 = s1_ref[block * 8 : block * 8 + 8, lanes]
                    o_ref[block * 128 + pair * 16 : block * 128 + pair * 16 + 16, lanes] = (
                        jnp.concatenate(
                            [c1 * picked[0] - s1 * picked[1], c1 * picked[2] - s1 * picked[3]],
                            axis=0,
                        ).astype(BF16)
                    )


def fourier_table():
    mu = jnp.arange(MUDIM, dtype=jnp.int32)
    lat = mu // 128 * 2 + mu // 64 % 2
    wave = (lat + LAT * (mu // 16 % 4 * TG + mu % TG))[None, :]
    quarter = (mu // 8 % 2 * (POINTS // 4))[None, :]
    origin = (jnp.arange(LON * NT, dtype=jnp.int32) // NT * NLOC)[:, None]
    local = jnp.arange(NPAD, dtype=jnp.int32)[:, None]
    first = ((wave * origin + quarter) % POINTS).astype(F32) * (2.0 * math.pi / POINTS)
    second = (wave * local % POINTS).astype(F32) * (2.0 * math.pi / POINTS)
    table = pl.pallas_call(
        table_kernel,
        out_shape=jax.ShapeDtypeStruct((KDIM, MUDIM), BF16),
        in_specs=[pl.BlockSpec(memory_space=pltpu.VMEM)] * 4,
        out_specs=pl.BlockSpec(memory_space=pltpu.VMEM),
        compiler_params=params(32),
        cost_estimate=cost(1e7, 4e6),
        name="fourier_table",
    )(
        jnp.cos(first),
        jnp.sin(first),
        jnp.where(local < NLOC, jnp.cos(second), 0.0),
        jnp.where(local < NLOC, jnp.sin(second), 0.0),
    )
    return table, wave


def fold_matrix(lat):
    row = jnp.arange(JALL, dtype=jnp.int32)[:, None]
    column = jnp.arange(JALL, dtype=jnp.int32)[None, :]
    odd, band, place = row // JHALF, row % JHALF // JPAD, row % JPAD
    sign = jnp.where((odd + lat) % 2 == 0, 1.0, -1.0)
    same = (row % JHALF == column) & (place < JLOC)
    mirror = (column // JPAD == LAT - 1 - band) & (column % JPAD == JLOC - 1 - place)
    return jnp.where(same, 1.0, jnp.where(mirror, sign, 0.0)).astype(BF16)


def swap(values, axis):
    return lax.all_to_all(values, axis, 0, 0, tiled=True)


def per_device(field, cotangent, spectral_filter):
    lat = lax.axis_index("lat")
    spacing = 2.0 * math.pi / POINTS
    table, wave = fourier_table()
    doubling = jnp.where(wave == 0, 1.0, 2.0).astype(F32)
    plain = jnp.ones((1, MUDIM), F32)
    theta = ((lat * JLOC + jnp.arange(JPAD)).astype(F32) + 0.5) * (math.pi / (JLOC * LAT))
    quadrature = jnp.broadcast_to(
        (spacing * math.pi / (JLOC * LAT) * jnp.sin(theta))[:, None], (JPAD, 128)
    )
    ones = jnp.ones((JPAD, 128), F32)
    tables = legendre_tables(lat)
    weights = jnp.transpose(
        spectral_filter.astype(F32).reshape(2, DEG // 2, 2, CH), (0, 3, 2, 1)
    )
    weights = jnp.pad(weights, ((0, 0), (0, 0), (0, 0), (0, (LPAD - DEG) // 2)))
    weights = weights.reshape(2, CH, LPAD)
    fold = fold_matrix(lat)
    weights = jnp.broadcast_to(weights[:, :, None, :], (2, CH, TG, LPAD))

    field_shares = swap(to_shares(field), "lon")
    cot_local, table = lax.optimization_barrier((to_shares(cotangent), table))
    cot_shares = swap(cot_local, "lon")
    field_local, tables, fold, weights = lax.optimization_barrier(
        (to_waves(field_shares, table, quadrature, plain), tables, fold, weights)
    )
    field_waves = swap(field_local, "lat")
    cot_waves = swap(to_waves(cot_shares, table, ones, doubling), "lat")

    analysis_shape = (GROUPS, 2, CH, TG, LPAD)
    analysis_block = (1, 2, CH, TG, LPAD)
    out_waves, analysis = spectral_stage(
        forward_kernel,
        GROUPS,
        tables,
        field_waves,
        weights,
        fold,
        [],
        [(pltpu.HBM(analysis_shape, F32), pl.BlockSpec(analysis_block, lambda g: (g, 0, 0, 0, 0)))],
        [],
    )
    (grad_waves,) = spectral_stage(
        backward_kernel,
        GROUPS + 2,
        tables,
        cot_waves,
        weights,
        fold,
        [
            (
                analysis,
                pl.BlockSpec(
                    analysis_block, lambda g: (jnp.minimum(g, GROUPS - 1), 0, 0, 0, 0)
                ),
            )
        ],
        [],
        [pltpu.VMEM((2, CH, TG, LPAD), F32)],
    )
    output_waves = swap(out_waves, "lat")
    grad_waves = swap(grad_waves, "lat")
    output = from_shares(swap(from_waves(output_waves, table, ones, doubling), "lon"))
    grad_field = from_shares(swap(from_waves(grad_waves, table, quadrature, plain), "lon"))
    summed = jnp.sum(grad_waves[:, GROUPS:].astype(F32), axis=0)
    summed = summed.reshape(2, LPAD // 128, CH, 128).transpose(0, 2, 1, 3)
    summed = summed.reshape(2, CH, 2, LHALF)[:, :, :, : DEG // 2]
    grad_filter = jnp.transpose(summed, (0, 3, 2, 1)).reshape(2, DEG, CH)
    return (output, grad_field, grad_filter)


def solution(mesh):
    in_specs = (P("lon", "lat", None), P("lon", "lat", None), P(None, None, "lon"))
    out_specs = (P("lon", "lat", None), P("lon", "lat", None), P(None, None, "lon"))
    return jax.shard_map(
        per_device, mesh=mesh, in_specs=in_specs, out_specs=out_specs, check_vma=False
    )
```

```python
import functools
import math

import jax
import jax.numpy as jnp
from jax import lax
from jax.experimental import pallas as pl
from jax.experimental.pallas import tpu as pltpu
from jax.sharding import PartitionSpec as P

LAT, LON = 16, 32
NLOC, JLOC = 45, 45
NPAD, JPAD = 48, 48
CH = 8
NT = NPAD // 16
KDIM = LON * NPAD
MUDIM = 1024
GROUPS, TG = 4, 8
HALF_GROUPS = GROUPS // 2
JALL = LAT * JPAD
JHALF = JALL // 2
DEG, LPAD = 720, 768
LHALF = LPAD // 2
POINTS = NLOC * LON
F32, BF16 = jnp.float32, jnp.bfloat16
MIB = 1 << 20


def transpose_blocks(tiles, width):
    count = len(tiles)
    lane = lax.broadcasted_iota(jnp.int32, tiles[0].shape, 1)
    block = lane // width

    def turn(value, shift):
        return pltpu.roll(value, shift, 1) if shift else value

    tiles = [turn(tile, n * width) for n, tile in enumerate(tiles)]
    step = 1
    while step < count:
        high = (block & step) != 0
        tiles = [jnp.where(high, tiles[(n + step) % count], tiles[n]) for n in range(count)]
        step *= 2
    return [turn(tiles[-k % count], (128 - k * width) % 128) for k in range(count)]


def hbm(value):
    return pltpu.with_memory_space_constraint(value, pltpu.HBM)


def cost(flops, size):
    return pl.CostEstimate(flops=int(flops), bytes_accessed=int(size), transcendentals=0)


def params(mib):
    return pltpu.CompilerParams(vmem_limit_bytes=mib * MIB)


BLOCKS = 8


def grids():
    shape = (8, 128)
    return lax.broadcasted_iota(jnp.int32, shape, 0), lax.broadcasted_iota(jnp.int32, shape, 1) // CH


def pack_tail(t0, t1, t2):
    row, slot = grids()
    lowered = pltpu.roll(t1, 5, 0)
    p = jnp.where(row < 5, t0, lowered)
    moved = jnp.where(slot == 13, pltpu.roll(lowered, 128 - 16, 1), t2)
    return p, jnp.where(row < 5, moved, pltpu.roll(t1, 2, 0))


def unpack_tail(p, q):
    row, slot = grids()
    moved = pltpu.roll(pltpu.roll(q, 3, 0), 16, 1)
    t1 = jnp.where(slot == 15, moved, pltpu.roll(q, 6, 0))
    return p, jnp.where(row < 3, pltpu.roll(p, 3, 0), t1), q


def fill_spare(tile, q, group):
    _, slot = grids()
    return jnp.where(slot >= 13, pltpu.roll(q, (13 - 3 * group) * CH, 1), tile)


def collect_spare(tiles):
    _, slot = grids()
    q = None
    for group, tile in enumerate(tiles):
        part = pltpu.roll(tile, 128 - (13 - 3 * group) * CH, 1)
        q = part if q is None else jnp.where(slot >= 3 * group, part, q)
    return q


def both(top, bottom):
    return jnp.concatenate([top, bottom], axis=0)


def unpack_block(read):
    b2, b5, b6, b7 = read(2), read(5), read(6), read(7)
    q = collect_spare([b2[:8], b2[8:], b5[:8], b5[8:], b7[:8]])
    t0, t1, t2 = unpack_tail(b7[8:], q)
    return both(b6[:8], t0), both(b6[8:], t1), both(b7[:8], t2)


def pack_block(tiles):
    p, q = pack_tail(tiles[0][8:], tiles[1][8:], tiles[2][8:])
    return both(tiles[0][:8], tiles[1][:8]), both(fill_spare(tiles[2][:8], q, 4), p), q


def fill_rows(tile, q, jr):
    return both(fill_spare(tile[:8], q, 2 * jr), fill_spare(tile[8:], q, 2 * jr + 1))


def share_kernel(x_ref, o_ref, tail_ref, q_ref):
    for h in range(2):
        lanes = slice(h * 128, h * 128 + 128)
        for jr in (2, 0, 1):
            count = min(16, JLOC - jr * 16)
            for nt in range(NT):
                tiles = []
                for n in range(nt * 16, nt * 16 + 16):
                    if n >= NLOC:
                        tiles.append(jnp.zeros((16, 128), F32))
                        continue
                    tile = x_ref[n, jr * 16 : jr * 16 + count, lanes].astype(F32)
                    if count < 16:
                        tile = jnp.concatenate([tile, jnp.zeros((16 - count, 128), F32)], axis=0)
                    tiles.append(tile)
                tiles = transpose_blocks(tiles, CH)
                for k in range(16):
                    if jr == 2:
                        tail_ref[nt, k] = tiles[k]
                        continue
                    tile = tiles[k]
                    if nt == 2:
                        tile = fill_rows(tile, q_ref[k], jr)
                    o_ref[h * 16 + k, jr * NT + nt] = tile.astype(BF16)
            if jr == 2:
                for k in range(16):
                    six, seven, q = pack_block([tail_ref[nt, k] for nt in range(NT)])
                    o_ref[h * 16 + k, 6] = six.astype(BF16)
                    o_ref[h * 16 + k, 7] = seven.astype(BF16)
                    q_ref[k] = q


def to_shares(grid):
    return pl.pallas_call(
        share_kernel,
        out_shape=pltpu.HBM((LON, BLOCKS, 16, 128), BF16),
        scratch_shapes=[pltpu.VMEM((NT, 16, 16, 128), F32), pltpu.VMEM((16, 8, 128), F32)],
        compiler_params=params(32),
        cost_estimate=cost(1e7, 2.4e6),
        name="to_shares",
    )(hbm(grid))


def unshare_kernel(x_ref, o_ref, tail_ref):
    for h in range(2):
        lanes = slice(h * 128, h * 128 + 128)
        for k in range(16):
            for nt, tile in enumerate(unpack_block(lambda b: x_ref[h * 16 + k, b].astype(F32))):
                tail_ref[nt, k] = tile
        for jr in range(3):
            count = min(16, JLOC - jr * 16)
            for nt in range(NT):
                if jr == 2:
                    tiles = [tail_ref[nt, k] for k in range(16)]
                else:
                    tiles = [x_ref[h * 16 + k, jr * NT + nt].astype(F32) for k in range(16)]
                tiles = transpose_blocks(tiles, CH)
                for n in range(min(16, NLOC - nt * 16)):
                    o_ref[nt * 16 + n, jr * 16 : jr * 16 + count, lanes] = tiles[n].astype(BF16)[
                        :count
                    ]


def from_shares(shares):
    return pl.pallas_call(
        unshare_kernel,
        out_shape=pltpu.HBM((NLOC, JLOC, 256), BF16),
        scratch_shapes=[pltpu.VMEM((NT, 16, 16, 128), F32)],
        compiler_params=params(32),
        cost_estimate=cost(1e7, 2.4e6),
        name="from_shares",
    )(shares)


ROUNDS = KDIM // 128 // NT


def message_tiles(part):
    return [((part * 8 + q) // NT, (part * 8 + q) % NT) for q in range(8)]


def x_rows(jr, c):
    return slice(jr * 128 + c * 16, jr * 128 + c * 16 + 16)


def fourier_kernel(x_ref, f_ref, row_ref, lane_ref, o_ref, xs_ref, ys_ref, tail_ref):
    @pl.loop(0, LON, unroll=8)
    def _(k):
        for nt, tile in enumerate(unpack_block(lambda b: x_ref[k, b].astype(F32))):
            tail_ref[k, nt] = tile

    @pl.loop(0, ROUNDS)
    def _(r):
        for jr in range(3):
            for part in range(NT):
                tiles = [
                    tail_ref[r * 8 + k, nt]
                    if jr == 2
                    else x_ref[r * 8 + k, jr * NT + nt].astype(F32)
                    for k, nt in message_tiles(part)
                ]
                tiles = transpose_blocks(tiles, 1)
                lanes = pl.ds(pl.multiple_of((r * NT + part) * 128, 128), 128)
                for c in range(8):
                    xs_ref[x_rows(jr, c), lanes] = tiles[c].astype(BF16)

    ys_ref[...] = jnp.dot(xs_ref[...], f_ref[...], preferred_element_type=F32)

    @pl.loop(0, 8, unroll=2)
    def _(ii):
        lanes = pl.ds(pl.multiple_of(ii * 128, 128), 128)
        for jr in range(3):
            rows = slice(jr * 16, jr * 16 + 16)
            scale = row_ref[rows, :] * lane_ref[:, lanes]
            tiles = [ys_ref[x_rows(jr, c), lanes] * scale for c in range(8)]
            tiles = transpose_blocks(tiles, 16)
            for i_lo in range(2):
                for g in range(GROUPS):
                    o_ref[ii * 2 + i_lo, g, rows, :] = tiles[i_lo * 4 + g].astype(BF16)


def to_waves(shares, table, row_scale, lane_scale):
    return pl.pallas_call(
        fourier_kernel,
        out_shape=pltpu.HBM((LAT, GROUPS, JPAD, 128), BF16),
        scratch_shapes=[
            pltpu.VMEM((CH * JPAD, KDIM), BF16),
            pltpu.VMEM((CH * JPAD, MUDIM), F32),
            pltpu.VMEM((LON, NT, 16, 128), F32),
        ],
        compiler_params=params(32),
        cost_estimate=cost(2 * 384 * KDIM * MUDIM, 5e6),
        name="to_waves",
    )(shares, hbm(table), row_scale, lane_scale)


def inverse_kernel(v_ref, f_ref, row_ref, lane_ref, o_ref, vs_ref, ys_ref, tail_ref, q_ref):
    @pl.loop(0, 8, unroll=2)
    def _(ii):
        lanes = pl.ds(pl.multiple_of(ii * 128, 128), 128)
        scale = lane_ref[:, lanes]
        for jr in range(3):
            rows = slice(jr * 16, jr * 16 + 16)
            tiles = [
                v_ref[ii * 2 + i_lo, g, rows, :].astype(F32)
                for i_lo in range(2)
                for g in range(GROUPS)
            ]
            tiles = transpose_blocks(tiles, 16)
            for c in range(8):
                vs_ref[x_rows(jr, c), lanes] = (tiles[c] * scale).astype(BF16)

    ys_ref[...] = lax.dot_general(
        vs_ref[...], f_ref[...], (((1,), (1,)), ((), ())), preferred_element_type=F32
    )

    def grid_tiles(r, jr, part):
        lanes = pl.ds(pl.multiple_of((r * NT + part) * 128, 128), 128)
        scale = row_ref[jr * 16 : jr * 16 + 16, :]
        tiles = [ys_ref[x_rows(jr, c), lanes] * scale for c in range(8)]
        tiles = transpose_blocks(tiles, 1)
        return tiles

    @pl.loop(0, ROUNDS)
    def _(r):
        for part in range(NT):
            for (k, nt), tile in zip(message_tiles(part), grid_tiles(r, 2, part)):
                tail_ref[r * 8 + k, nt] = tile

    @pl.loop(0, LON, unroll=8)
    def _(k):
        six, seven, q = pack_block([tail_ref[k, nt] for nt in range(NT)])
        o_ref[k, 6] = six.astype(BF16)
        o_ref[k, 7] = seven.astype(BF16)
        q_ref[k] = q

    @pl.loop(0, ROUNDS)
    def _(r):
        for jr in range(2):
            for part in range(NT):
                for (k, nt), tile in zip(message_tiles(part), grid_tiles(r, jr, part)):
                    if nt == 2:
                        tile = fill_rows(tile, q_ref[r * 8 + k], jr)
                    o_ref[r * 8 + k, jr * NT + nt] = tile.astype(BF16)


def from_waves(waves, table, row_scale, lane_scale):
    return pl.pallas_call(
        inverse_kernel,
        out_shape=pltpu.HBM((LON, BLOCKS, 16, 128), BF16),
        scratch_shapes=[
            pltpu.VMEM((CH * JPAD, MUDIM), BF16),
            pltpu.VMEM((CH * JPAD, KDIM), F32),
            pltpu.VMEM((LON, NT, 16, 128), F32),
            pltpu.VMEM((LON, 8, 128), F32),
        ],
        compiler_params=params(32),
        cost_estimate=cost(2 * 384 * KDIM * MUDIM, 5e6),
        name="from_waves",
    )(waves, hbm(table), row_scale, lane_scale)


LCHUNK = 128


def legendre_kernel(first, m_ref, f_ref, h_ref, x_ref, p0_ref, e0_ref, o_ref, p1_s, p2_s, e_s, rows_s):
    g, lc = pl.program_id(0) + first, pl.program_id(1)

    @pl.when(lc == 0)
    def _():
        p1_s[...] = jnp.zeros_like(p1_s)
        p2_s[...] = jnp.zeros_like(p2_s)
        e_s[...] = e0_ref[0]

    @pl.when(lc < g)
    def _():
        o_ref[...] = jnp.zeros_like(o_ref)

    def chunk(starts):
        x = jnp.broadcast_to(x_ref[...], (TG, JHALF))
        orders = jnp.broadcast_to(m_ref[0][:, :1], (TG, JHALF))
        p1, p2, e = p1_s[...], p2_s[...], e_s[...]
        for u in range(LCHUNK):
            if u % 8 == 0:
                big = jnp.abs(p1) > 2.0**24
                down = jnp.where(big, 2.0**-48, 1.0)
                p1, p2 = p1 * down, p2 * down
                e = jnp.where(big, e + 48.0, e)
                scale = jnp.exp2(jnp.maximum(e, -200.0))
            new = (f_ref[0][:, u : u + 1] * x) * p1 - h_ref[0][:, u : u + 1] * p2
            if starts:
                degree = (lc * LCHUNK + u).astype(F32)
                new = jnp.where(orders == degree, p0_ref[0], new)
            p1, p2 = new, p1
            value = new * scale
            for b in range(JHALF // 128):
                rows_s[b, u * TG : u * TG + TG, :] = value[:, b * 128 : b * 128 + 128]
        p1_s[...] = p1
        p2_s[...] = p2
        e_s[...] = e
        for t in range(TG):
            for odd in range(2):
                for b in range(JHALF // 128):
                    o_ref[t, odd, :, b * 128 : b * 128 + 128] = rows_s[
                        b, pl.ds(odd * TG + t, LCHUNK // 2, stride=2 * TG), :
                    ].astype(BF16)

    pl.when(lc == g)(functools.partial(chunk, True))
    pl.when(lc > g)(functools.partial(chunk, False))


def legendre_tables(lat, first):
    order = (lat + LAT * (first * TG + jnp.arange(HALF_GROUPS * TG, dtype=jnp.int32))).astype(F32)
    order = order[:, None]
    degrees = jnp.arange(LPAD, dtype=F32)[None, :]

    def factor_at(degree):
        inside = degree > order
        top = jnp.where(inside, 4.0 * degree * degree - 1.0, 1.0)
        low = jnp.where(inside, degree * degree - order * order, 1.0)
        return jnp.sqrt(top / low), inside

    factor, inside = factor_at(degrees)
    earlier, earlier_inside = factor_at(degrees - 1.0)
    forward = jnp.where(inside, factor, 0.0).reshape(HALF_GROUPS, TG, LPAD)
    back = jnp.where(earlier_inside, factor / earlier, 0.0).reshape(HALF_GROUPS, TG, LPAD)
    start_log = 0.5 * (
        lax.lgamma(order + 1.5) - lax.lgamma(jnp.float32(1.5)) - lax.lgamma(order + 1.0)
    ) - 0.5 * math.log(4.0 * math.pi)
    place = jnp.arange(JHALF, dtype=jnp.int32)
    cycle = place // JPAD * JLOC + jnp.minimum(place % JPAD, JLOC - 1)
    theta = (cycle.astype(F32) + 0.5) * (math.pi / (JLOC * LAT))
    start = (start_log + order * jnp.log(jnp.sin(theta))[None, :]) * (1.0 / math.log(2.0))
    exponent = jnp.floor(start)
    real = (place % JPAD < JLOC)[None, :]
    mantissa = jnp.where(real, jnp.exp2(start - exponent), 0.0)
    orders = jnp.broadcast_to(order, (HALF_GROUPS * TG, 128)).reshape(HALF_GROUPS, TG, 128)
    return pl.pallas_call(
        functools.partial(legendre_kernel, first),
        grid=(HALF_GROUPS, LPAD // LCHUNK),
        out_shape=pltpu.HBM((HALF_GROUPS * TG, 2, LHALF, JHALF), BF16),
        in_specs=[
            pl.BlockSpec((1, TG, 128), lambda g, lc: (g, 0, 0)),
            pl.BlockSpec((1, TG, LCHUNK), lambda g, lc: (g, 0, lc)),
            pl.BlockSpec((1, TG, LCHUNK), lambda g, lc: (g, 0, lc)),
            pl.BlockSpec((1, JHALF), lambda g, lc: (0, 0)),
            pl.BlockSpec((1, TG, JHALF), lambda g, lc: (g, 0, 0)),
            pl.BlockSpec((1, TG, JHALF), lambda g, lc: (g, 0, 0)),
        ],
        out_specs=pl.BlockSpec((TG, 2, LCHUNK // 2, JHALF), lambda g, lc: (g, 0, lc, 0)),
        scratch_shapes=[pltpu.VMEM((TG, JHALF), F32)] * 3
        + [pltpu.VMEM((JHALF // 128, LCHUNK * TG, 128), F32)],
        compiler_params=params(32),
        cost_estimate=cost(1.5e10 if first == 0 else 1e10, 1e7),
        name="legendre_tables",
    )(
        orders,
        forward,
        back,
        jnp.cos(theta)[None, :],
        mantissa.reshape(HALF_GROUPS, TG, JHALF),
        exponent.reshape(HALF_GROUPS, TG, JHALF),
    )


def spectral_body(low_ref, high_ref, z_ref, w_ref, fold_ref, sign, o_ref, s_ref, k_ref, u_ref):
    lane = lax.broadcasted_iota(jnp.int32, (JHALF, 128), 1) % TG
    row = lax.broadcasted_iota(jnp.int32, (128, LHALF), 0) % TG
    z = z_ref[:, 0].reshape(JALL, 128)
    folded = jnp.dot(fold_ref[...], z, preferred_element_type=F32)

    def products(g):
        first = 64 * g
        p_ref = low_ref if g < HALF_GROUPS else high_ref
        for odd in range(2):
            half = folded[odd * JHALF : odd * JHALF + JHALF]
            total = jnp.dot(
                jnp.concatenate([p_ref[t, odd, first:, :] for t in range(TG)], axis=1),
                jnp.concatenate(
                    [jnp.where(lane == t, half, 0.0).astype(BF16) for t in range(TG)], axis=0
                ),
                preferred_element_type=F32,
            )
            if first:
                s_ref[odd * LHALF : odd * LHALF + first, :] = jnp.zeros((first, 128), F32)
            s_ref[odd * LHALF + first : odd * LHALF + LHALF, :] = total

    def back_products(g):
        first = g // 2 * 128
        p_ref = low_ref if g < HALF_GROUPS else high_ref
        for odd in range(2):
            half = k_ref[:, odd * LHALF + first : odd * LHALF + LHALF]
            total = jnp.dot(
                jnp.concatenate(
                    [jnp.where(row[:, first:] == t, half, 0.0).astype(BF16) for t in range(TG)],
                    axis=1,
                ),
                jnp.concatenate([p_ref[t, odd, first:, :] for t in range(TG)], axis=0),
                preferred_element_type=F32,
            )
            u_ref[:, odd * JHALF : odd * JHALF + JHALF] = total.astype(BF16)

    for g in range(GROUPS):
        pl.when(pl.program_id(0) == g)(functools.partial(products, g))
    found = s_ref[...].T.reshape(CH, 2, TG, LPAD)
    real, imag = found[:, 0], found[:, 1]
    cross = w_ref[1] * sign
    kept = jnp.stack([w_ref[0] * real - cross * imag, w_ref[0] * imag + cross * real], axis=1)
    k_ref[...] = kept.reshape(128, LPAD)
    for g in range(GROUPS):
        pl.when(pl.program_id(0) == g)(functools.partial(back_products, g))
    spread = jnp.dot(u_ref[...], fold_ref[...], preferred_element_type=F32)
    o_ref[:, 0] = spread.T.astype(BF16).reshape(LAT, JPAD, 128)
    return real, imag


def forward_kernel(low_ref, high_ref, z_ref, w_ref, fold_ref, o_ref, a_ref, *scratch):
    real, imag = spectral_body(low_ref, high_ref, z_ref, w_ref, fold_ref, 1.0, o_ref, *scratch)
    a_ref[0, 0] = real
    a_ref[0, 1] = imag


def backward_kernel(low_ref, high_ref, z_ref, w_ref, fold_ref, a_ref, o_ref, g_ref, *scratch):
    step = pl.program_id(0)

    @pl.when(step == 0)
    def _():
        g_ref[...] = jnp.zeros_like(g_ref)

    @pl.when(step < GROUPS)
    def _():
        real, imag = spectral_body(low_ref, high_ref, z_ref, w_ref, fold_ref, -1.0, o_ref, *scratch)
        first, second = a_ref[0, 0], a_ref[0, 1]
        g_ref[0] += first * real + second * imag
        g_ref[1] += first * imag - second * real

    for part in range(2):

        @pl.when(step == GROUPS + part)
        def _():
            total = jnp.sum(g_ref[part], axis=1)
            rows = [total[:, b * 128 : b * 128 + 128] for b in range(LPAD // 128)]
            o_ref[:, 0] = jnp.broadcast_to(
                jnp.concatenate(rows, axis=0).astype(BF16)[None], (LAT, JPAD, 128)
            )


def spectral_stage(kernel, steps, tables, spectra, weights, fold, extra_in, extra_out, extra_scratch):
    last = GROUPS - 1
    return pl.pallas_call(
        kernel,
        grid=(steps,),
        out_shape=[pltpu.HBM((LAT, steps, JPAD, 128), BF16)] + [value for value, _ in extra_out],
        in_specs=[
            pl.BlockSpec(
                (TG, 2, LHALF, JHALF), lambda g: (jnp.minimum(g, HALF_GROUPS - 1), 0, 0, 0)
            ),
            pl.BlockSpec(
                (TG, 2, LHALF, JHALF),
                lambda g: (jnp.clip(g - HALF_GROUPS, 0, HALF_GROUPS - 1), 0, 0, 0),
            ),
            pl.BlockSpec((LAT, 1, JPAD, 128), lambda g: (0, jnp.minimum(g, last), 0, 0)),
            pl.BlockSpec((2, CH, TG, LPAD), lambda g: (0, 0, 0, 0)),
            pl.BlockSpec((JALL, JALL), lambda g: (0, 0)),
        ]
        + [spec for _, spec in extra_in],
        out_specs=[pl.BlockSpec((LAT, 1, JPAD, 128), lambda g: (0, g, 0, 0))]
        + [spec for _, spec in extra_out],
        scratch_shapes=extra_scratch
        + [
            pltpu.VMEM((LPAD, 128), F32),
            pltpu.VMEM((128, LPAD), F32),
            pltpu.VMEM((128, JALL), BF16),
        ],
        compiler_params=params(48),
        cost_estimate=cost(1.2e10, 2.2e7),
        name="spectral_stage",
    )(*tables, spectra, weights, hbm(fold), *[hbm(value) for value, _ in extra_in])


def table_kernel(c1_ref, s1_ref, c2_ref, s2_ref, o_ref):
    @pl.loop(0, MUDIM // 128)
    def _(lc):
        lanes = pl.ds(pl.multiple_of(lc * 128, 128), 128)
        row = lax.broadcasted_iota(jnp.int32, (8, 128), 0)
        for start in range(NT):
            part = (row + 2 * start) % NT
            for pair in range(8):
                picked = []
                for n in (2 * pair, 2 * pair + 1):
                    for ref in (c2_ref, s2_ref):
                        rows = [
                            jnp.broadcast_to(ref[nt * 16 + n : nt * 16 + n + 1, lanes], (8, 128))
                            for nt in range(NT)
                        ]
                        picked.append(
                            jnp.where(part == 0, rows[0], jnp.where(part == 1, rows[1], rows[2]))
                        )
                for block in range(start, KDIM // 128, NT):
                    c1 = c1_ref[block * 8 : block * 8 + 8, lanes]
                    s1 = s1_ref[block * 8 : block * 8 + 8, lanes]
                    o_ref[block * 128 + pair * 16 : block * 128 + pair * 16 + 16, lanes] = (
                        jnp.concatenate(
                            [c1 * picked[0] - s1 * picked[1], c1 * picked[2] - s1 * picked[3]],
                            axis=0,
                        ).astype(BF16)
                    )


def fourier_table():
    mu = jnp.arange(MUDIM, dtype=jnp.int32)
    lat = mu // 128 * 2 + mu // 64 % 2
    wave = (lat + LAT * (mu // 16 % 4 * TG + mu % TG))[None, :]
    quarter = (mu // 8 % 2 * (POINTS // 4))[None, :]
    origin = (jnp.arange(LON * NT, dtype=jnp.int32) // NT * NLOC)[:, None]
    local = jnp.arange(NPAD, dtype=jnp.int32)[:, None]
    first = ((wave * origin + quarter) % POINTS).astype(F32) * (2.0 * math.pi / POINTS)
    second = (wave * local % POINTS).astype(F32) * (2.0 * math.pi / POINTS)
    table = pl.pallas_call(
        table_kernel,
        out_shape=pltpu.HBM((KDIM, MUDIM), BF16),
        compiler_params=params(32),
        cost_estimate=cost(1e7, 4e6),
        name="fourier_table",
    )(
        jnp.cos(first),
        jnp.sin(first),
        jnp.where(local < NLOC, jnp.cos(second), 0.0),
        jnp.where(local < NLOC, jnp.sin(second), 0.0),
    )
    return table, wave


def fold_matrix(lat):
    row = jnp.arange(JALL, dtype=jnp.int32)[:, None]
    column = jnp.arange(JALL, dtype=jnp.int32)[None, :]
    odd, band, place = row // JHALF, row % JHALF // JPAD, row % JPAD
    sign = jnp.where((odd + lat) % 2 == 0, 1.0, -1.0)
    same = (row % JHALF == column) & (place < JLOC)
    mirror = (column // JPAD == LAT - 1 - band) & (column % JPAD == JLOC - 1 - place)
    return jnp.where(same, 1.0, jnp.where(mirror, sign, 0.0)).astype(BF16)


def swap(values, axis):
    return lax.all_to_all(values, axis, 0, 0, tiled=True)


def per_device(field, cotangent, spectral_filter):
    lat = lax.axis_index("lat")
    spacing = 2.0 * math.pi / POINTS
    table, wave = fourier_table()
    doubling = jnp.where(wave == 0, 1.0, 2.0).astype(F32)
    plain = jnp.ones((1, MUDIM), F32)
    theta = ((lat * JLOC + jnp.arange(JPAD)).astype(F32) + 0.5) * (math.pi / (JLOC * LAT))
    quadrature = jnp.broadcast_to(
        (spacing * math.pi / (JLOC * LAT) * jnp.sin(theta))[:, None], (JPAD, 128)
    )
    ones = jnp.ones((JPAD, 128), F32)
    low_tables = legendre_tables(lat, 0)
    high_tables = legendre_tables(lat, HALF_GROUPS)
    weights = jnp.transpose(
        spectral_filter.astype(F32).reshape(2, DEG // 2, 2, CH), (0, 3, 2, 1)
    )
    weights = jnp.pad(weights, ((0, 0), (0, 0), (0, 0), (0, (LPAD - DEG) // 2)))
    weights = weights.reshape(2, CH, LPAD)
    fold = fold_matrix(lat)
    weights = jnp.broadcast_to(weights[:, :, None, :], (2, CH, TG, LPAD))

    field_shares = swap(to_shares(field), "lon")
    cot_local, table, low_tables, fold, weights = lax.optimization_barrier(
        (to_shares(cotangent), table, low_tables, fold, weights)
    )
    field_waves = swap(to_waves(field_shares, table, quadrature, plain), "lat")
    field_waves, cot_local, high_tables = lax.optimization_barrier(
        (field_waves, cot_local, high_tables)
    )
    tables = (low_tables, high_tables)
    cot_shares = swap(cot_local, "lon")

    analysis_shape = (GROUPS, 2, CH, TG, LPAD)
    analysis_block = (1, 2, CH, TG, LPAD)
    out_waves, analysis = spectral_stage(
        forward_kernel,
        GROUPS,
        tables,
        field_waves,
        weights,
        fold,
        [],
        [(pltpu.HBM(analysis_shape, F32), pl.BlockSpec(analysis_block, lambda g: (g, 0, 0, 0, 0)))],
        [],
    )
    output_waves = swap(out_waves, "lat")
    cot_local, output_waves = lax.optimization_barrier(
        (to_waves(cot_shares, table, ones, doubling), output_waves)
    )
    cot_waves = swap(cot_local, "lat")
    output_local, cot_waves = lax.optimization_barrier(
        (from_waves(output_waves, table, ones, doubling), cot_waves)
    )
    output_shares = swap(output_local, "lon")
    (grad_waves,) = spectral_stage(
        backward_kernel,
        GROUPS + 2,
        tables,
        cot_waves,
        weights,
        fold,
        [
            (
                analysis,
                pl.BlockSpec(
                    analysis_block, lambda g: (jnp.minimum(g, GROUPS - 1), 0, 0, 0, 0)
                ),
            )
        ],
        [],
        [pltpu.VMEM((2, CH, TG, LPAD), F32)],
    )
    grad_waves, output_shares = lax.optimization_barrier((grad_waves, output_shares))
    grad_waves = swap(grad_waves, "lat")
    output = from_shares(output_shares)
    grad_field = from_shares(swap(from_waves(grad_waves, table, quadrature, plain), "lon"))
    summed = jnp.sum(grad_waves[:, GROUPS:].astype(F32), axis=0)
    summed = summed.reshape(2, LPAD // 128, CH, 128).transpose(0, 2, 1, 3)
    summed = summed.reshape(2, CH, 2, LHALF)[:, :, :, : DEG // 2]
    grad_filter = jnp.transpose(summed, (0, 3, 2, 1)).reshape(2, DEG, CH)
    return (output, grad_field, grad_filter)


def solution(mesh):
    in_specs = (P("lon", "lat", None), P("lon", "lat", None), P(None, None, "lon"))
    out_specs = (P("lon", "lat", None), P("lon", "lat", None), P(None, None, "lon"))
    return jax.shard_map(
        per_device, mesh=mesh, in_specs=in_specs, out_specs=out_specs, check_vma=False
    )
```

```python
import functools
import math

import jax
import jax.numpy as jnp
from jax import lax
from jax.experimental import pallas as pl
from jax.experimental.pallas import tpu as pltpu
from jax.sharding import PartitionSpec as P

LAT, LON = 16, 32
NLOC, JLOC = 45, 45
NPAD, JPAD = 48, 48
CH = 8
NT = NPAD // 16
KDIM = LON * NPAD
MUDIM = 1024
GROUPS, TG = 4, 8
HALF_GROUPS = GROUPS // 2
JALL = LAT * JPAD
JHALF = JALL // 2
DEG, LPAD = 720, 768
LHALF = LPAD // 2
POINTS = NLOC * LON
F32, BF16 = jnp.float32, jnp.bfloat16
MIB = 1 << 20


def transpose_blocks(tiles, width):
    count = len(tiles)
    lane = lax.broadcasted_iota(jnp.int32, tiles[0].shape, 1)
    block = lane // width

    def turn(value, shift):
        return pltpu.roll(value, shift, 1) if shift else value

    tiles = [turn(tile, n * width) for n, tile in enumerate(tiles)]
    step = 1
    while step < count:
        high = (block & step) != 0
        tiles = [jnp.where(high, tiles[(n + step) % count], tiles[n]) for n in range(count)]
        step *= 2
    return [turn(tiles[-k % count], (128 - k * width) % 128) for k in range(count)]


def hbm(value):
    return pltpu.with_memory_space_constraint(value, pltpu.HBM)


def cost(flops, size):
    return pl.CostEstimate(flops=int(flops), bytes_accessed=int(size), transcendentals=0)


def params(mib):
    return pltpu.CompilerParams(vmem_limit_bytes=mib * MIB)


BLOCKS = 8


def grids():
    shape = (8, 128)
    return lax.broadcasted_iota(jnp.int32, shape, 0), lax.broadcasted_iota(jnp.int32, shape, 1) // CH


def pack_tail(t0, t1, t2):
    row, slot = grids()
    lowered = pltpu.roll(t1, 5, 0)
    p = jnp.where(row < 5, t0, lowered)
    moved = jnp.where(slot == 13, pltpu.roll(lowered, 128 - 16, 1), t2)
    return p, jnp.where(row < 5, moved, pltpu.roll(t1, 2, 0))


def unpack_tail(p, q):
    row, slot = grids()
    moved = pltpu.roll(pltpu.roll(q, 3, 0), 16, 1)
    t1 = jnp.where(slot == 15, moved, pltpu.roll(q, 6, 0))
    return p, jnp.where(row < 3, pltpu.roll(p, 3, 0), t1), q


def fill_spare(tile, q, group):
    _, slot = grids()
    return jnp.where(slot >= 13, pltpu.roll(q, (13 - 3 * group) * CH, 1), tile)


def collect_spare(tiles):
    _, slot = grids()
    q = None
    for group, tile in enumerate(tiles):
        part = pltpu.roll(tile, 128 - (13 - 3 * group) * CH, 1)
        q = part if q is None else jnp.where(slot >= 3 * group, part, q)
    return q


def both(top, bottom):
    return jnp.concatenate([top, bottom], axis=0)


def unpack_block(read):
    b2, b5, b6, b7 = read(2), read(5), read(6), read(7)
    q = collect_spare([b2[:8], b2[8:], b5[:8], b5[8:], b7[:8]])
    t0, t1, t2 = unpack_tail(b7[8:], q)
    return both(b6[:8], t0), both(b6[8:], t1), both(b7[:8], t2)


def pack_block(tiles):
    p, q = pack_tail(tiles[0][8:], tiles[1][8:], tiles[2][8:])
    return both(tiles[0][:8], tiles[1][:8]), both(fill_spare(tiles[2][:8], q, 4), p), q


def fill_rows(tile, q, jr):
    return both(fill_spare(tile[:8], q, 2 * jr), fill_spare(tile[8:], q, 2 * jr + 1))


def share_kernel(x_ref, o_ref, tail_ref, q_ref):
    for h in range(2):
        lanes = slice(h * 128, h * 128 + 128)
        for jr in (2, 0, 1):
            count = min(16, JLOC - jr * 16)
            for nt in range(NT):
                tiles = []
                for n in range(nt * 16, nt * 16 + 16):
                    if n >= NLOC:
                        tiles.append(jnp.zeros((16, 128), F32))
                        continue
                    tile = x_ref[n, jr * 16 : jr * 16 + count, lanes].astype(F32)
                    if count < 16:
                        tile = jnp.concatenate([tile, jnp.zeros((16 - count, 128), F32)], axis=0)
                    tiles.append(tile)
                tiles = transpose_blocks(tiles, CH)
                for k in range(16):
                    if jr == 2:
                        tail_ref[nt, k] = tiles[k]
                        continue
                    tile = tiles[k]
                    if nt == 2:
                        tile = fill_rows(tile, q_ref[k], jr)
                    o_ref[h * 16 + k, jr * NT + nt] = tile.astype(BF16)
            if jr == 2:
                for k in range(16):
                    six, seven, q = pack_block([tail_ref[nt, k] for nt in range(NT)])
                    o_ref[h * 16 + k, 6] = six.astype(BF16)
                    o_ref[h * 16 + k, 7] = seven.astype(BF16)
                    q_ref[k] = q


def to_shares(grid):
    return pl.pallas_call(
        share_kernel,
        out_shape=pltpu.HBM((LON, BLOCKS, 16, 128), BF16),
        scratch_shapes=[pltpu.VMEM((NT, 16, 16, 128), F32), pltpu.VMEM((16, 8, 128), F32)],
        compiler_params=params(32),
        cost_estimate=cost(1e7, 2.4e6),
        name="to_shares",
    )(hbm(grid))


def unshare_kernel(x_ref, o_ref, tail_ref):
    for h in range(2):
        lanes = slice(h * 128, h * 128 + 128)
        for k in range(16):
            for nt, tile in enumerate(unpack_block(lambda b: x_ref[h * 16 + k, b].astype(F32))):
                tail_ref[nt, k] = tile
        for jr in range(3):
            count = min(16, JLOC - jr * 16)
            for nt in range(NT):
                if jr == 2:
                    tiles = [tail_ref[nt, k] for k in range(16)]
                else:
                    tiles = [x_ref[h * 16 + k, jr * NT + nt].astype(F32) for k in range(16)]
                tiles = transpose_blocks(tiles, CH)
                for n in range(min(16, NLOC - nt * 16)):
                    o_ref[nt * 16 + n, jr * 16 : jr * 16 + count, lanes] = tiles[n].astype(BF16)[
                        :count
                    ]


def from_shares(shares):
    return pl.pallas_call(
        unshare_kernel,
        out_shape=pltpu.HBM((NLOC, JLOC, 256), BF16),
        scratch_shapes=[pltpu.VMEM((NT, 16, 16, 128), F32)],
        compiler_params=params(32),
        cost_estimate=cost(1e7, 2.4e6),
        name="from_shares",
    )(shares)


ROUNDS = KDIM // 128 // NT


def message_tiles(part):
    return [((part * 8 + q) // NT, (part * 8 + q) % NT) for q in range(8)]


def x_rows(jr, c):
    return slice(jr * 128 + c * 16, jr * 128 + c * 16 + 16)


def fourier_kernel(x_ref, f_ref, row_ref, lane_ref, o_ref, xs_ref, ys_ref, tail_ref):
    @pl.loop(0, LON, unroll=8)
    def _(k):
        for nt, tile in enumerate(unpack_block(lambda b: x_ref[k, b].astype(F32))):
            tail_ref[k, nt] = tile

    @pl.loop(0, ROUNDS)
    def _(r):
        for jr in range(3):
            for part in range(NT):
                tiles = [
                    tail_ref[r * 8 + k, nt]
                    if jr == 2
                    else x_ref[r * 8 + k, jr * NT + nt].astype(F32)
                    for k, nt in message_tiles(part)
                ]
                tiles = transpose_blocks(tiles, 1)
                lanes = pl.ds(pl.multiple_of((r * NT + part) * 128, 128), 128)
                for c in range(8):
                    xs_ref[x_rows(jr, c), lanes] = tiles[c].astype(BF16)

    ys_ref[...] = jnp.dot(xs_ref[...], f_ref[...], preferred_element_type=F32)

    @pl.loop(0, 8, unroll=2)
    def _(ii):
        lanes = pl.ds(pl.multiple_of(ii * 128, 128), 128)
        for jr in range(3):
            rows = slice(jr * 16, jr * 16 + 16)
            scale = row_ref[rows, :] * lane_ref[:, lanes]
            tiles = [ys_ref[x_rows(jr, c), lanes] * scale for c in range(8)]
            tiles = transpose_blocks(tiles, 16)
            for i_lo in range(2):
                for g in range(GROUPS):
                    o_ref[ii * 2 + i_lo, g, rows, :] = tiles[i_lo * 4 + g].astype(BF16)


def to_waves(shares, table, row_scale, lane_scale):
    return pl.pallas_call(
        fourier_kernel,
        out_shape=pltpu.HBM((LAT, GROUPS, JPAD, 128), BF16),
        scratch_shapes=[
            pltpu.VMEM((CH * JPAD, KDIM), BF16),
            pltpu.VMEM((CH * JPAD, MUDIM), F32),
            pltpu.VMEM((LON, NT, 16, 128), F32),
        ],
        compiler_params=params(32),
        cost_estimate=cost(2 * 384 * KDIM * MUDIM, 5e6),
        name="to_waves",
    )(shares, hbm(table), row_scale, lane_scale)


def inverse_kernel(v_ref, f_ref, row_ref, lane_ref, o_ref, vs_ref, ys_ref, tail_ref, q_ref):
    @pl.loop(0, 8, unroll=2)
    def _(ii):
        lanes = pl.ds(pl.multiple_of(ii * 128, 128), 128)
        scale = lane_ref[:, lanes]
        for jr in range(3):
            rows = slice(jr * 16, jr * 16 + 16)
            tiles = [
                v_ref[ii * 2 + i_lo, g, rows, :].astype(F32)
                for i_lo in range(2)
                for g in range(GROUPS)
            ]
            tiles = transpose_blocks(tiles, 16)
            for c in range(8):
                vs_ref[x_rows(jr, c), lanes] = (tiles[c] * scale).astype(BF16)

    ys_ref[...] = lax.dot_general(
        vs_ref[...], f_ref[...], (((1,), (1,)), ((), ())), preferred_element_type=F32
    )

    def grid_tiles(r, jr, part):
        lanes = pl.ds(pl.multiple_of((r * NT + part) * 128, 128), 128)
        scale = row_ref[jr * 16 : jr * 16 + 16, :]
        tiles = [ys_ref[x_rows(jr, c), lanes] * scale for c in range(8)]
        tiles = transpose_blocks(tiles, 1)
        return tiles

    @pl.loop(0, ROUNDS)
    def _(r):
        for part in range(NT):
            for (k, nt), tile in zip(message_tiles(part), grid_tiles(r, 2, part)):
                tail_ref[r * 8 + k, nt] = tile

    @pl.loop(0, LON, unroll=8)
    def _(k):
        six, seven, q = pack_block([tail_ref[k, nt] for nt in range(NT)])
        o_ref[k, 6] = six.astype(BF16)
        o_ref[k, 7] = seven.astype(BF16)
        q_ref[k] = q

    @pl.loop(0, ROUNDS)
    def _(r):
        for jr in range(2):
            for part in range(NT):
                for (k, nt), tile in zip(message_tiles(part), grid_tiles(r, jr, part)):
                    if nt == 2:
                        tile = fill_rows(tile, q_ref[r * 8 + k], jr)
                    o_ref[r * 8 + k, jr * NT + nt] = tile.astype(BF16)


def from_waves(waves, table, row_scale, lane_scale):
    return pl.pallas_call(
        inverse_kernel,
        out_shape=pltpu.HBM((LON, BLOCKS, 16, 128), BF16),
        scratch_shapes=[
            pltpu.VMEM((CH * JPAD, MUDIM), BF16),
            pltpu.VMEM((CH * JPAD, KDIM), F32),
            pltpu.VMEM((LON, NT, 16, 128), F32),
            pltpu.VMEM((LON, 8, 128), F32),
        ],
        compiler_params=params(32),
        cost_estimate=cost(2 * 384 * KDIM * MUDIM, 5e6),
        name="from_waves",
    )(waves, hbm(table), row_scale, lane_scale)


LCHUNK = 128


def legendre_kernel(first, m_ref, f_ref, h_ref, x_ref, p0_ref, e0_ref, *rest):
    o_ref, p1_s, p2_s, e_s, rows_s = rest[-5:]
    g, lc = pl.program_id(0) + first, pl.program_id(1)

    @pl.when(lc == 0)
    def _():
        p1_s[...] = jnp.zeros_like(p1_s)
        p2_s[...] = jnp.zeros_like(p2_s)
        e_s[...] = e0_ref[0]

    @pl.when(lc < g)
    def _():
        o_ref[...] = jnp.zeros_like(o_ref)

    def chunk(starts):
        x = jnp.broadcast_to(x_ref[...], (TG, JHALF))
        orders = jnp.broadcast_to(m_ref[0][:, :1], (TG, JHALF))
        p1, p2, e = p1_s[...], p2_s[...], e_s[...]
        for u in range(LCHUNK):
            if u % 8 == 0:
                big = jnp.abs(p1) > 2.0**24
                down = jnp.where(big, 2.0**-48, 1.0)
                p1, p2 = p1 * down, p2 * down
                e = jnp.where(big, e + 48.0, e)
                scale = jnp.exp2(jnp.maximum(e, -200.0))
            new = (f_ref[0][:, u : u + 1] * x) * p1 - h_ref[0][:, u : u + 1] * p2
            if starts:
                degree = (lc * LCHUNK + u).astype(F32)
                new = jnp.where(orders == degree, p0_ref[0], new)
            p1, p2 = new, p1
            value = new * scale
            for b in range(JHALF // 128):
                rows_s[b, u * TG : u * TG + TG, :] = value[:, b * 128 : b * 128 + 128]
        p1_s[...] = p1
        p2_s[...] = p2
        e_s[...] = e
        for t in range(TG):
            for odd in range(2):
                for b in range(JHALF // 128):
                    o_ref[t, odd, :, b * 128 : b * 128 + 128] = rows_s[
                        b, pl.ds(odd * TG + t, LCHUNK // 2, stride=2 * TG), :
                    ].astype(BF16)

    pl.when(lc == g)(functools.partial(chunk, True))
    pl.when(lc > g)(functools.partial(chunk, False))


def legendre_tables(lat, first, earlier_half=None):
    held = [] if earlier_half is None else [earlier_half]
    order = (lat + LAT * (first * TG + jnp.arange(HALF_GROUPS * TG, dtype=jnp.int32))).astype(F32)
    order = order[:, None]
    degrees = jnp.arange(LPAD, dtype=F32)[None, :]

    def factor_at(degree):
        inside = degree > order
        top = jnp.where(inside, 4.0 * degree * degree - 1.0, 1.0)
        low = jnp.where(inside, degree * degree - order * order, 1.0)
        return jnp.sqrt(top / low), inside

    factor, inside = factor_at(degrees)
    earlier, earlier_inside = factor_at(degrees - 1.0)
    forward = jnp.where(inside, factor, 0.0).reshape(HALF_GROUPS, TG, LPAD)
    back = jnp.where(earlier_inside, factor / earlier, 0.0).reshape(HALF_GROUPS, TG, LPAD)
    start_log = 0.5 * (
        lax.lgamma(order + 1.5) - lax.lgamma(jnp.float32(1.5)) - lax.lgamma(order + 1.0)
    ) - 0.5 * math.log(4.0 * math.pi)
    place = jnp.arange(JHALF, dtype=jnp.int32)
    cycle = place // JPAD * JLOC + jnp.minimum(place % JPAD, JLOC - 1)
    theta = (cycle.astype(F32) + 0.5) * (math.pi / (JLOC * LAT))
    start = (start_log + order * jnp.log(jnp.sin(theta))[None, :]) * (1.0 / math.log(2.0))
    exponent = jnp.floor(start)
    real = (place % JPAD < JLOC)[None, :]
    mantissa = jnp.where(real, jnp.exp2(start - exponent), 0.0)
    orders = jnp.broadcast_to(order, (HALF_GROUPS * TG, 128)).reshape(HALF_GROUPS, TG, 128)
    return pl.pallas_call(
        functools.partial(legendre_kernel, first),
        grid=(HALF_GROUPS, LPAD // LCHUNK),
        out_shape=pltpu.HBM((GROUPS * TG, 2, LHALF, JHALF), BF16),
        in_specs=[
            pl.BlockSpec((1, TG, 128), lambda g, lc: (g, 0, 0)),
            pl.BlockSpec((1, TG, LCHUNK), lambda g, lc: (g, 0, lc)),
            pl.BlockSpec((1, TG, LCHUNK), lambda g, lc: (g, 0, lc)),
            pl.BlockSpec((1, JHALF), lambda g, lc: (0, 0)),
            pl.BlockSpec((1, TG, JHALF), lambda g, lc: (g, 0, 0)),
            pl.BlockSpec((1, TG, JHALF), lambda g, lc: (g, 0, 0)),
        ]
        + [pl.BlockSpec(memory_space=pl.ANY)] * len(held),
        out_specs=pl.BlockSpec(
            (TG, 2, LCHUNK // 2, JHALF), lambda g, lc: (g + first, 0, lc, 0)
        ),
        input_output_aliases={6: 0} if held else {},
        scratch_shapes=[pltpu.VMEM((TG, JHALF), F32)] * 3
        + [pltpu.VMEM((JHALF // 128, LCHUNK * TG, 128), F32)],
        compiler_params=params(32),
        cost_estimate=cost(1.5e10 if first == 0 else 1e10, 1e7),
        name="legendre_tables",
    )(
        orders,
        forward,
        back,
        jnp.cos(theta)[None, :],
        mantissa.reshape(HALF_GROUPS, TG, JHALF),
        exponent.reshape(HALF_GROUPS, TG, JHALF),
        *held,
    )


def spectral_body(p_ref, z_ref, w_ref, fold_ref, sign, o_ref, s_ref, k_ref, u_ref):
    lane = lax.broadcasted_iota(jnp.int32, (JHALF, 128), 1) % TG
    row = lax.broadcasted_iota(jnp.int32, (128, LHALF), 0) % TG
    z = z_ref[:, 0].reshape(JALL, 128)
    folded = jnp.dot(fold_ref[...], z, preferred_element_type=F32)

    def products(g):
        first = 64 * g
        for odd in range(2):
            half = folded[odd * JHALF : odd * JHALF + JHALF]
            total = jnp.dot(
                jnp.concatenate([p_ref[t, odd, first:, :] for t in range(TG)], axis=1),
                jnp.concatenate(
                    [jnp.where(lane == t, half, 0.0).astype(BF16) for t in range(TG)], axis=0
                ),
                preferred_element_type=F32,
            )
            if first:
                s_ref[odd * LHALF : odd * LHALF + first, :] = jnp.zeros((first, 128), F32)
            s_ref[odd * LHALF + first : odd * LHALF + LHALF, :] = total

    def back_products(g):
        first = g // 2 * 128
        for odd in range(2):
            half = k_ref[:, odd * LHALF + first : odd * LHALF + LHALF]
            total = jnp.dot(
                jnp.concatenate(
                    [jnp.where(row[:, first:] == t, half, 0.0).astype(BF16) for t in range(TG)],
                    axis=1,
                ),
                jnp.concatenate([p_ref[t, odd, first:, :] for t in range(TG)], axis=0),
                preferred_element_type=F32,
            )
            u_ref[:, odd * JHALF : odd * JHALF + JHALF] = total.astype(BF16)

    for g in range(GROUPS):
        pl.when(pl.program_id(0) == g)(functools.partial(products, g))
    found = s_ref[...].T.reshape(CH, 2, TG, LPAD)
    real, imag = found[:, 0], found[:, 1]
    cross = w_ref[1] * sign
    kept = jnp.stack([w_ref[0] * real - cross * imag, w_ref[0] * imag + cross * real], axis=1)
    k_ref[...] = kept.reshape(128, LPAD)
    for g in range(GROUPS):
        pl.when(pl.program_id(0) == g)(functools.partial(back_products, g))
    spread = jnp.dot(u_ref[...], fold_ref[...], preferred_element_type=F32)
    o_ref[:, 0] = spread.astype(BF16).T.reshape(LAT, JPAD, 128)
    return real, imag


def forward_kernel(p_ref, z_ref, w_ref, fold_ref, o_ref, a_ref, *scratch):
    real, imag = spectral_body(p_ref, z_ref, w_ref, fold_ref, 1.0, o_ref, *scratch)
    a_ref[0, 0] = real
    a_ref[0, 1] = imag


def backward_kernel(p_ref, z_ref, w_ref, fold_ref, a_ref, o_ref, g_ref, *scratch):
    step = pl.program_id(0)

    @pl.when(step == 0)
    def _():
        g_ref[...] = jnp.zeros_like(g_ref)

    @pl.when(step < GROUPS)
    def _():
        real, imag = spectral_body(p_ref, z_ref, w_ref, fold_ref, -1.0, o_ref, *scratch)
        first, second = a_ref[0, 0], a_ref[0, 1]
        g_ref[0] += first * real + second * imag
        g_ref[1] += first * imag - second * real

    for part in range(2):

        @pl.when(step == GROUPS + part)
        def _():
            total = jnp.sum(g_ref[part], axis=1)
            rows = [total[:, b * 128 : b * 128 + 128] for b in range(LPAD // 128)]
            o_ref[:, 0] = jnp.broadcast_to(
                jnp.concatenate(rows, axis=0).astype(BF16)[None], (LAT, JPAD, 128)
            )


def spectral_stage(kernel, steps, tables, spectra, weights, fold, extra_in, extra_out, extra_scratch):
    last = GROUPS - 1
    return pl.pallas_call(
        kernel,
        grid=(steps,),
        out_shape=[pltpu.HBM((LAT, steps, JPAD, 128), BF16)] + [value for value, _ in extra_out],
        in_specs=[
            pl.BlockSpec((TG, 2, LHALF, JHALF), lambda g: (jnp.minimum(g, last), 0, 0, 0)),
            pl.BlockSpec((LAT, 1, JPAD, 128), lambda g: (0, jnp.minimum(g, last), 0, 0)),
            pl.BlockSpec((2, CH, TG, LPAD), lambda g: (0, 0, 0, 0)),
            pl.BlockSpec((JALL, JALL), lambda g: (0, 0)),
        ]
        + [spec for _, spec in extra_in],
        out_specs=[pl.BlockSpec((LAT, 1, JPAD, 128), lambda g: (0, g, 0, 0))]
        + [spec for _, spec in extra_out],
        scratch_shapes=extra_scratch
        + [
            pltpu.VMEM((LPAD, 128), F32),
            pltpu.VMEM((128, LPAD), F32),
            pltpu.VMEM((128, JALL), BF16),
        ],
        compiler_params=params(48),
        cost_estimate=cost(1.2e10, 2.2e7),
        name="spectral_stage",
    )(tables, spectra, weights, hbm(fold), *[hbm(value) for value, _ in extra_in])


def table_kernel(c1_ref, s1_ref, c2_ref, s2_ref, o_ref):
    @pl.loop(0, MUDIM // 128)
    def _(lc):
        lanes = pl.ds(pl.multiple_of(lc * 128, 128), 128)
        row = lax.broadcasted_iota(jnp.int32, (8, 128), 0)
        for start in range(NT):
            part = (row + 2 * start) % NT
            for pair in range(8):
                picked = []
                for n in (2 * pair, 2 * pair + 1):
                    for ref in (c2_ref, s2_ref):
                        rows = [
                            jnp.broadcast_to(ref[nt * 16 + n : nt * 16 + n + 1, lanes], (8, 128))
                            for nt in range(NT)
                        ]
                        picked.append(
                            jnp.where(part == 0, rows[0], jnp.where(part == 1, rows[1], rows[2]))
                        )
                for block in range(start, KDIM // 128, NT):
                    c1 = c1_ref[block * 8 : block * 8 + 8, lanes]
                    s1 = s1_ref[block * 8 : block * 8 + 8, lanes]
                    o_ref[block * 128 + pair * 16 : block * 128 + pair * 16 + 16, lanes] = (
                        jnp.concatenate(
                            [c1 * picked[0] - s1 * picked[1], c1 * picked[2] - s1 * picked[3]],
                            axis=0,
                        ).astype(BF16)
                    )


def fourier_table():
    mu = jnp.arange(MUDIM, dtype=jnp.int32)
    lat = mu // 128 * 2 + mu // 64 % 2
    wave = (lat + LAT * (mu // 16 % 4 * TG + mu % TG))[None, :]
    quarter = (mu // 8 % 2 * (POINTS // 4))[None, :]
    origin = (jnp.arange(LON * NT, dtype=jnp.int32) // NT * NLOC)[:, None]
    local = jnp.arange(NPAD, dtype=jnp.int32)[:, None]
    first = ((wave * origin + quarter) % POINTS).astype(F32) * (2.0 * math.pi / POINTS)
    second = (wave * local % POINTS).astype(F32) * (2.0 * math.pi / POINTS)
    table = pl.pallas_call(
        table_kernel,
        out_shape=pltpu.HBM((KDIM, MUDIM), BF16),
        compiler_params=params(32),
        cost_estimate=cost(1e7, 4e6),
        name="fourier_table",
    )(
        jnp.cos(first),
        jnp.sin(first),
        jnp.where(local < NLOC, jnp.cos(second), 0.0),
        jnp.where(local < NLOC, jnp.sin(second), 0.0),
    )
    return table, wave


def fold_matrix(lat):
    row = jnp.arange(JALL, dtype=jnp.int32)[:, None]
    column = jnp.arange(JALL, dtype=jnp.int32)[None, :]
    odd, band, place = row // JHALF, row % JHALF // JPAD, row % JPAD
    sign = jnp.where((odd + lat) % 2 == 0, 1.0, -1.0)
    same = (row % JHALF == column) & (place < JLOC)
    mirror = (column // JPAD == LAT - 1 - band) & (column % JPAD == JLOC - 1 - place)
    return jnp.where(same, 1.0, jnp.where(mirror, sign, 0.0)).astype(BF16)


def swap(values, axis):
    return lax.all_to_all(values, axis, 0, 0, tiled=True)


def per_device(field, cotangent, spectral_filter):
    lat = lax.axis_index("lat")
    spacing = 2.0 * math.pi / POINTS
    table, wave = fourier_table()
    doubling = jnp.where(wave == 0, 1.0, 2.0).astype(F32)
    plain = jnp.ones((1, MUDIM), F32)
    theta = ((lat * JLOC + jnp.arange(JPAD)).astype(F32) + 0.5) * (math.pi / (JLOC * LAT))
    quadrature = jnp.broadcast_to(
        (spacing * math.pi / (JLOC * LAT) * jnp.sin(theta))[:, None], (JPAD, 128)
    )
    ones = jnp.ones((JPAD, 128), F32)
    low_tables = legendre_tables(lat, 0)
    weights = jnp.transpose(
        spectral_filter.astype(F32).reshape(2, DEG // 2, 2, CH), (0, 3, 2, 1)
    )
    weights = jnp.pad(weights, ((0, 0), (0, 0), (0, 0), (0, (LPAD - DEG) // 2)))
    weights = weights.reshape(2, CH, LPAD)
    fold = fold_matrix(lat)
    weights = jnp.broadcast_to(weights[:, :, None, :], (2, CH, TG, LPAD))

    field_shares = swap(to_shares(field), "lon")
    cot_local, table, low_tables = lax.optimization_barrier(
        (to_shares(cotangent), table, low_tables)
    )
    cot_shares = swap(cot_local, "lon")
    tables = legendre_tables(lat, HALF_GROUPS, low_tables)
    field_local, tables, fold, weights = lax.optimization_barrier(
        (to_waves(field_shares, table, quadrature, plain), tables, fold, weights)
    )
    field_waves = swap(field_local, "lat")
    cot_waves = swap(to_waves(cot_shares, table, ones, doubling), "lat")

    analysis_shape = (GROUPS, 2, CH, TG, LPAD)
    analysis_block = (1, 2, CH, TG, LPAD)
    out_waves, analysis = spectral_stage(
        forward_kernel,
        GROUPS,
        tables,
        field_waves,
        weights,
        fold,
        [],
        [(pltpu.HBM(analysis_shape, F32), pl.BlockSpec(analysis_block, lambda g: (g, 0, 0, 0, 0)))],
        [],
    )
    (grad_waves,) = spectral_stage(
        backward_kernel,
        GROUPS + 2,
        tables,
        cot_waves,
        weights,
        fold,
        [
            (
                analysis,
                pl.BlockSpec(
                    analysis_block, lambda g: (jnp.minimum(g, GROUPS - 1), 0, 0, 0, 0)
                ),
            )
        ],
        [],
        [pltpu.VMEM((2, CH, TG, LPAD), F32)],
    )
    output_waves = swap(out_waves, "lat")
    grad_waves = swap(grad_waves, "lat")
    output = from_shares(swap(from_waves(output_waves, table, ones, doubling), "lon"))
    grad_field = from_shares(swap(from_waves(grad_waves, table, quadrature, plain), "lon"))
    summed = jnp.sum(grad_waves[:, GROUPS:].astype(F32), axis=0)
    summed = summed.reshape(2, LPAD // 128, CH, 128).transpose(0, 2, 1, 3)
    summed = summed.reshape(2, CH, 2, LHALF)[:, :, :, : DEG // 2]
    grad_filter = jnp.transpose(summed, (0, 3, 2, 1)).reshape(2, DEG, CH)
    return (output, grad_field, grad_filter)


def solution(mesh):
    in_specs = (P("lon", "lat", None), P("lon", "lat", None), P(None, None, "lon"))
    out_specs = (P("lon", "lat", None), P("lon", "lat", None), P(None, None, "lon"))
    return jax.shard_map(
        per_device, mesh=mesh, in_specs=in_specs, out_specs=out_specs, check_vma=False
    )
```

```python
import functools
import math

import jax
import jax.numpy as jnp
from jax import lax
from jax.experimental import pallas as pl
from jax.experimental.pallas import tpu as pltpu
from jax.sharding import PartitionSpec as P

LAT, LON = 16, 32
NLOC, JLOC = 45, 45
NPAD, JPAD = 48, 48
CH = 8
NT = NPAD // 16
KDIM = LON * NPAD
MUDIM = 1024
GROUPS, TG = 4, 8
HALF_GROUPS = GROUPS // 2
JALL = LAT * JPAD
JHALF = JALL // 2
DEG, LPAD = 720, 768
LHALF = LPAD // 2
POINTS = NLOC * LON
F32, BF16 = jnp.float32, jnp.bfloat16
MIB = 1 << 20


def transpose_blocks(tiles, width):
    count = len(tiles)
    lane = lax.broadcasted_iota(jnp.int32, tiles[0].shape, 1)
    block = lane // width

    def turn(value, shift):
        return pltpu.roll(value, shift, 1) if shift else value

    tiles = [turn(tile, n * width) for n, tile in enumerate(tiles)]
    step = 1
    while step < count:
        high = (block & step) != 0
        tiles = [jnp.where(high, tiles[(n + step) % count], tiles[n]) for n in range(count)]
        step *= 2
    return [turn(tiles[-k % count], (128 - k * width) % 128) for k in range(count)]


def hbm(value):
    return pltpu.with_memory_space_constraint(value, pltpu.HBM)


def cost(flops, size):
    return pl.CostEstimate(flops=int(flops), bytes_accessed=int(size), transcendentals=0)


def params(mib):
    return pltpu.CompilerParams(vmem_limit_bytes=mib * MIB)


BLOCKS = 8


def grids():
    shape = (8, 128)
    return lax.broadcasted_iota(jnp.int32, shape, 0), lax.broadcasted_iota(jnp.int32, shape, 1) // CH


def pack_tail(t0, t1, t2):
    row, slot = grids()
    lowered = pltpu.roll(t1, 5, 0)
    p = jnp.where(row < 5, t0, lowered)
    moved = jnp.where(slot == 13, pltpu.roll(lowered, 128 - 16, 1), t2)
    return p, jnp.where(row < 5, moved, pltpu.roll(t1, 2, 0))


def unpack_tail(p, q):
    row, slot = grids()
    moved = pltpu.roll(pltpu.roll(q, 3, 0), 16, 1)
    t1 = jnp.where(slot == 15, moved, pltpu.roll(q, 6, 0))
    return p, jnp.where(row < 3, pltpu.roll(p, 3, 0), t1), q


def fill_spare(tile, q, group):
    _, slot = grids()
    return jnp.where(slot >= 13, pltpu.roll(q, (13 - 3 * group) * CH, 1), tile)


def collect_spare(tiles):
    _, slot = grids()
    q = None
    for group, tile in enumerate(tiles):
        part = pltpu.roll(tile, 128 - (13 - 3 * group) * CH, 1)
        q = part if q is None else jnp.where(slot >= 3 * group, part, q)
    return q


def both(top, bottom):
    return jnp.concatenate([top, bottom], axis=0)


def unpack_block(read):
    b2, b5, b6, b7 = read(2), read(5), read(6), read(7)
    q = collect_spare([b2[:8], b2[8:], b5[:8], b5[8:], b7[:8]])
    t0, t1, t2 = unpack_tail(b7[8:], q)
    return both(b6[:8], t0), both(b6[8:], t1), both(b7[:8], t2)


def pack_block(tiles):
    p, q = pack_tail(tiles[0][8:], tiles[1][8:], tiles[2][8:])
    return both(tiles[0][:8], tiles[1][:8]), both(fill_spare(tiles[2][:8], q, 4), p), q


def fill_rows(tile, q, jr):
    return both(fill_spare(tile[:8], q, 2 * jr), fill_spare(tile[8:], q, 2 * jr + 1))


def share_kernel(x_ref, o_ref, tail_ref, q_ref):
    for h in range(2):
        lanes = slice(h * 128, h * 128 + 128)
        for jr in (2, 0, 1):
            count = min(16, JLOC - jr * 16)
            for nt in range(NT):
                tiles = []
                for n in range(nt * 16, nt * 16 + 16):
                    if n >= NLOC:
                        tiles.append(jnp.zeros((16, 128), F32))
                        continue
                    tile = x_ref[n, jr * 16 : jr * 16 + count, lanes].astype(F32)
                    if count < 16:
                        tile = jnp.concatenate([tile, jnp.zeros((16 - count, 128), F32)], axis=0)
                    tiles.append(tile)
                tiles = transpose_blocks(tiles, CH)
                for k in range(16):
                    if jr == 2:
                        tail_ref[nt, k] = tiles[k]
                        continue
                    tile = tiles[k]
                    if nt == 2:
                        tile = fill_rows(tile, q_ref[k], jr)
                    o_ref[h * 16 + k, jr * NT + nt] = tile.astype(BF16)
            if jr == 2:
                for k in range(16):
                    six, seven, q = pack_block([tail_ref[nt, k] for nt in range(NT)])
                    o_ref[h * 16 + k, 6] = six.astype(BF16)
                    o_ref[h * 16 + k, 7] = seven.astype(BF16)
                    q_ref[k] = q


def to_shares(grid):
    return pl.pallas_call(
        share_kernel,
        out_shape=pltpu.HBM((LON, BLOCKS, 16, 128), BF16),
        scratch_shapes=[pltpu.VMEM((NT, 16, 16, 128), F32), pltpu.VMEM((16, 8, 128), F32)],
        compiler_params=params(32),
        cost_estimate=cost(1e7, 2.4e6),
        name="to_shares",
    )(hbm(grid))


def unshare_kernel(x_ref, o_ref, tail_ref):
    for h in range(2):
        lanes = slice(h * 128, h * 128 + 128)
        for k in range(16):
            for nt, tile in enumerate(unpack_block(lambda b: x_ref[h * 16 + k, b].astype(F32))):
                tail_ref[nt, k] = tile
        for jr in range(3):
            count = min(16, JLOC - jr * 16)
            for nt in range(NT):
                if jr == 2:
                    tiles = [tail_ref[nt, k] for k in range(16)]
                else:
                    tiles = [x_ref[h * 16 + k, jr * NT + nt].astype(F32) for k in range(16)]
                tiles = transpose_blocks(tiles, CH)
                for n in range(min(16, NLOC - nt * 16)):
                    o_ref[nt * 16 + n, jr * 16 : jr * 16 + count, lanes] = tiles[n].astype(BF16)[
                        :count
                    ]


def from_shares(shares):
    return pl.pallas_call(
        unshare_kernel,
        out_shape=pltpu.HBM((NLOC, JLOC, 256), BF16),
        scratch_shapes=[pltpu.VMEM((NT, 16, 16, 128), F32)],
        compiler_params=params(32),
        cost_estimate=cost(1e7, 2.4e6),
        name="from_shares",
    )(shares)


ROUNDS = KDIM // 128 // NT


def message_tiles(part):
    return [((part * 8 + q) // NT, (part * 8 + q) % NT) for q in range(8)]


def x_rows(jr, c):
    return slice(jr * 128 + c * 16, jr * 128 + c * 16 + 16)


def fourier_kernel(x_ref, f_ref, row_ref, lane_ref, o_ref, xs_ref, ys_ref, tail_ref):
    @pl.loop(0, LON, unroll=8)
    def _(k):
        for nt, tile in enumerate(unpack_block(lambda b: x_ref[k, b].astype(F32))):
            tail_ref[k, nt] = tile

    @pl.loop(0, ROUNDS)
    def _(r):
        for jr in range(3):
            for part in range(NT):
                tiles = [
                    tail_ref[r * 8 + k, nt]
                    if jr == 2
                    else x_ref[r * 8 + k, jr * NT + nt].astype(F32)
                    for k, nt in message_tiles(part)
                ]
                tiles = transpose_blocks(tiles, 1)
                lanes = pl.ds(pl.multiple_of((r * NT + part) * 128, 128), 128)
                for c in range(8):
                    xs_ref[x_rows(jr, c), lanes] = tiles[c].astype(BF16)

    ys_ref[...] = jnp.dot(xs_ref[...], f_ref[...], preferred_element_type=F32)

    @pl.loop(0, 8, unroll=2)
    def _(ii):
        lanes = pl.ds(pl.multiple_of(ii * 128, 128), 128)
        for jr in range(3):
            rows = slice(jr * 16, jr * 16 + 16)
            scale = row_ref[rows, :] * lane_ref[:, lanes]
            tiles = [ys_ref[x_rows(jr, c), lanes] * scale for c in range(8)]
            tiles = transpose_blocks(tiles, 16)
            for i_lo in range(2):
                for g in range(GROUPS):
                    o_ref[ii * 2 + i_lo, g, rows, :] = tiles[i_lo * 4 + g].astype(BF16)


def to_waves(shares, table, row_scale, lane_scale):
    return pl.pallas_call(
        fourier_kernel,
        out_shape=pltpu.HBM((LAT, GROUPS, JPAD, 128), BF16),
        scratch_shapes=[
            pltpu.VMEM((CH * JPAD, KDIM), BF16),
            pltpu.VMEM((CH * JPAD, MUDIM), F32),
            pltpu.VMEM((LON, NT, 16, 128), F32),
        ],
        compiler_params=params(32),
        cost_estimate=cost(2 * 384 * KDIM * MUDIM, 5e6),
        name="to_waves",
    )(shares, hbm(table), row_scale, lane_scale)


def inverse_kernel(v_ref, f_ref, row_ref, lane_ref, o_ref, vs_ref, ys_ref, tail_ref, q_ref):
    @pl.loop(0, 8, unroll=2)
    def _(ii):
        lanes = pl.ds(pl.multiple_of(ii * 128, 128), 128)
        scale = lane_ref[:, lanes]
        for jr in range(3):
            rows = slice(jr * 16, jr * 16 + 16)
            tiles = [
                v_ref[ii * 2 + i_lo, g, rows, :].astype(F32)
                for i_lo in range(2)
                for g in range(GROUPS)
            ]
            tiles = transpose_blocks(tiles, 16)
            for c in range(8):
                vs_ref[x_rows(jr, c), lanes] = (tiles[c] * scale).astype(BF16)

    ys_ref[...] = lax.dot_general(
        vs_ref[...], f_ref[...], (((1,), (1,)), ((), ())), preferred_element_type=F32
    )

    def grid_tiles(r, jr, part):
        lanes = pl.ds(pl.multiple_of((r * NT + part) * 128, 128), 128)
        scale = row_ref[jr * 16 : jr * 16 + 16, :]
        tiles = [ys_ref[x_rows(jr, c), lanes] * scale for c in range(8)]
        tiles = transpose_blocks(tiles, 1)
        return tiles

    @pl.loop(0, ROUNDS)
    def _(r):
        for part in range(NT):
            for (k, nt), tile in zip(message_tiles(part), grid_tiles(r, 2, part)):
                tail_ref[r * 8 + k, nt] = tile

    @pl.loop(0, LON, unroll=8)
    def _(k):
        six, seven, q = pack_block([tail_ref[k, nt] for nt in range(NT)])
        o_ref[k, 6] = six.astype(BF16)
        o_ref[k, 7] = seven.astype(BF16)
        q_ref[k] = q

    @pl.loop(0, ROUNDS)
    def _(r):
        for jr in range(2):
            for part in range(NT):
                for (k, nt), tile in zip(message_tiles(part), grid_tiles(r, jr, part)):
                    if nt == 2:
                        tile = fill_rows(tile, q_ref[r * 8 + k], jr)
                    o_ref[r * 8 + k, jr * NT + nt] = tile.astype(BF16)


def from_waves(waves, table, row_scale, lane_scale):
    return pl.pallas_call(
        inverse_kernel,
        out_shape=pltpu.HBM((LON, BLOCKS, 16, 128), BF16),
        scratch_shapes=[
            pltpu.VMEM((CH * JPAD, MUDIM), BF16),
            pltpu.VMEM((CH * JPAD, KDIM), F32),
            pltpu.VMEM((LON, NT, 16, 128), F32),
            pltpu.VMEM((LON, 8, 128), F32),
        ],
        compiler_params=params(32),
        cost_estimate=cost(2 * 384 * KDIM * MUDIM, 5e6),
        name="from_waves",
    )(waves, hbm(table), row_scale, lane_scale)


LCHUNK = 128


def legendre_kernel(first, m_ref, f_ref, h_ref, x_ref, p0_ref, e0_ref, *rest):
    o_ref, p1_s, p2_s, e_s, rows_s = rest[-5:]
    g, lc = pl.program_id(0) + first, pl.program_id(1)

    @pl.when(lc == 0)
    def _():
        p1_s[...] = jnp.zeros_like(p1_s)
        p2_s[...] = jnp.zeros_like(p2_s)
        e_s[...] = e0_ref[0]

    @pl.when(lc < g)
    def _():
        o_ref[...] = jnp.zeros_like(o_ref)

    def chunk(starts):
        x = jnp.broadcast_to(x_ref[...], (TG, JHALF))
        orders = jnp.broadcast_to(m_ref[0][:, :1], (TG, JHALF))
        p1, p2, e = p1_s[...], p2_s[...], e_s[...]
        for u in range(LCHUNK):
            if u % 8 == 0:
                big = jnp.abs(p1) > 2.0**24
                down = jnp.where(big, 2.0**-48, 1.0)
                p1, p2 = p1 * down, p2 * down
                e = jnp.where(big, e + 48.0, e)
                scale = jnp.exp2(jnp.maximum(e, -200.0))
            new = (f_ref[0][:, u : u + 1] * x) * p1 - h_ref[0][:, u : u + 1] * p2
            if starts:
                degree = (lc * LCHUNK + u).astype(F32)
                new = jnp.where(orders == degree, p0_ref[0], new)
            p1, p2 = new, p1
            value = new * scale
            for b in range(JHALF // 128):
                rows_s[b, u * TG : u * TG + TG, :] = value[:, b * 128 : b * 128 + 128]
        p1_s[...] = p1
        p2_s[...] = p2
        e_s[...] = e
        for t in range(TG):
            for odd in range(2):
                for b in range(JHALF // 128):
                    o_ref[t, odd, :, b * 128 : b * 128 + 128] = rows_s[
                        b, pl.ds(odd * TG + t, LCHUNK // 2, stride=2 * TG), :
                    ].astype(BF16)

    pl.when(lc == g)(functools.partial(chunk, True))
    pl.when(lc > g)(functools.partial(chunk, False))


def legendre_tables(lat, first, earlier_half=None):
    held = [] if earlier_half is None else [earlier_half]
    order = (lat + LAT * (first * TG + jnp.arange(HALF_GROUPS * TG, dtype=jnp.int32))).astype(F32)
    order = order[:, None]
    degrees = jnp.arange(LPAD, dtype=F32)[None, :]

    def factor_at(degree):
        inside = degree > order
        top = jnp.where(inside, 4.0 * degree * degree - 1.0, 1.0)
        low = jnp.where(inside, degree * degree - order * order, 1.0)
        return jnp.sqrt(top / low), inside

    factor, inside = factor_at(degrees)
    earlier, earlier_inside = factor_at(degrees - 1.0)
    forward = jnp.where(inside, factor, 0.0).reshape(HALF_GROUPS, TG, LPAD)
    back = jnp.where(earlier_inside, factor / earlier, 0.0).reshape(HALF_GROUPS, TG, LPAD)
    start_log = 0.5 * (
        lax.lgamma(order + 1.5) - lax.lgamma(jnp.float32(1.5)) - lax.lgamma(order + 1.0)
    ) - 0.5 * math.log(4.0 * math.pi)
    place = jnp.arange(JHALF, dtype=jnp.int32)
    cycle = place // JPAD * JLOC + jnp.minimum(place % JPAD, JLOC - 1)
    theta = (cycle.astype(F32) + 0.5) * (math.pi / (JLOC * LAT))
    start = (start_log + order * jnp.log(jnp.sin(theta))[None, :]) * (1.0 / math.log(2.0))
    exponent = jnp.floor(start)
    real = (place % JPAD < JLOC)[None, :]
    mantissa = jnp.where(real, jnp.exp2(start - exponent), 0.0)
    orders = jnp.broadcast_to(order, (HALF_GROUPS * TG, 128)).reshape(HALF_GROUPS, TG, 128)
    return pl.pallas_call(
        functools.partial(legendre_kernel, first),
        grid=(HALF_GROUPS, LPAD // LCHUNK),
        out_shape=pltpu.HBM((GROUPS * TG, 2, LHALF, JHALF), BF16),
        in_specs=[
            pl.BlockSpec((1, TG, 128), lambda g, lc: (g, 0, 0)),
            pl.BlockSpec((1, TG, LCHUNK), lambda g, lc: (g, 0, lc)),
            pl.BlockSpec((1, TG, LCHUNK), lambda g, lc: (g, 0, lc)),
            pl.BlockSpec((1, JHALF), lambda g, lc: (0, 0)),
            pl.BlockSpec((1, TG, JHALF), lambda g, lc: (g, 0, 0)),
            pl.BlockSpec((1, TG, JHALF), lambda g, lc: (g, 0, 0)),
        ]
        + [pl.BlockSpec(memory_space=pl.ANY)] * len(held),
        out_specs=pl.BlockSpec(
            (TG, 2, LCHUNK // 2, JHALF), lambda g, lc: (g + first, 0, lc, 0)
        ),
        input_output_aliases={6: 0} if held else {},
        scratch_shapes=[pltpu.VMEM((TG, JHALF), F32)] * 3
        + [pltpu.VMEM((JHALF // 128, LCHUNK * TG, 128), F32)],
        compiler_params=params(32),
        cost_estimate=cost(1.5e10 if first == 0 else 1e10, 1e7),
        name="legendre_tables",
    )(
        orders,
        forward,
        back,
        jnp.cos(theta)[None, :],
        mantissa.reshape(HALF_GROUPS, TG, JHALF),
        exponent.reshape(HALF_GROUPS, TG, JHALF),
        *held,
    )


def spectral_body(p_hbm, z_ref, w_ref, fold_ref, sign, o_ref, done, p_ref, h_ref, sems):
    lane = lax.broadcasted_iota(jnp.int32, (JHALF, 128), 1) % TG
    row = lax.broadcasted_iota(jnp.int32, (128, LHALF), 0) % TG

    def fetch(g):
        part = (pl.ds(g * TG, TG), slice(None), pl.ds(g // 2 * 128, LHALF - g // 2 * 128))
        return pltpu.make_async_copy(p_hbm.at[part], p_ref.at[part], sems.at[g])

    def analyse(g):
        first = 64 * g
        start = g // 2 * 128
        found = []
        for odd in range(2):
            half = h_ref[g, odd]
            total = jnp.dot(
                jnp.concatenate([p_ref[g * TG + t, odd, first:, :] for t in range(TG)], axis=1),
                jnp.concatenate(
                    [jnp.where(lane == t, half, 0.0).astype(BF16) for t in range(TG)], axis=0
                ),
                preferred_element_type=F32,
            )
            if first > start:
                total = jnp.concatenate([jnp.zeros((first - start, 128), F32), total], axis=0)
            found.append(total)
        return found

    def synthesise(g, found):
        start = g // 2 * 128
        halves = []
        for odd in range(2):
            columns = slice(odd * LHALF + start, odd * LHALF + LHALF)
            size = LHALF - start
            value = found[odd].T.reshape(CH, 2, TG, size)
            real, imag = value[:, 0], value[:, 1]
            done(g, real, imag, columns)
            direct, cross = w_ref[0, :, :, columns], w_ref[1, :, :, columns] * sign
            kept = jnp.stack(
                [direct * real - cross * imag, direct * imag + cross * real], axis=1
            ).reshape(128, size)
            total = jnp.dot(
                jnp.concatenate(
                    [jnp.where(row[:, start:] == t, kept, 0.0).astype(BF16) for t in range(TG)],
                    axis=1,
                ),
                jnp.concatenate([p_ref[g * TG + t, odd, start:, :] for t in range(TG)], axis=0),
                preferred_element_type=F32,
            )
            halves.append(total)
        mirrored = jnp.dot(
            (halves[0] - halves[1]).astype(BF16), fold_ref[...], preferred_element_type=F32
        )
        north, south = (halves[0] + halves[1]).astype(BF16), mirrored.astype(BF16)
        o_ref[: LAT // 2, g] = north.T.reshape(LAT // 2, JPAD, 128)
        o_ref[LAT // 2 :, g] = south.T.reshape(LAT // 2, JPAD, 128)

    order = list(reversed(range(GROUPS)))
    for g in order:
        fetch(g).start()
    south = jnp.concatenate(
        [z_ref[LAT // 2 :, g].reshape(JHALF, 128) for g in range(GROUPS)], axis=1
    )
    mirrored = jnp.dot(fold_ref[...], south, preferred_element_type=F32)
    for g in range(GROUPS):
        north = z_ref[: LAT // 2, g].reshape(JHALF, 128).astype(F32)
        h_ref[g, 0] = north + mirrored[:, g * 128 : g * 128 + 128]
        h_ref[g, 1] = north - mirrored[:, g * 128 : g * 128 + 128]
    held = None
    for g in order:
        fetch(g).wait()
        found = analyse(g)
        if held is not None:
            synthesise(*held)
        held = (g, found)
    synthesise(*held)


def forward_kernel(p_hbm, z_ref, w_ref, fold_ref, o_ref, a_ref, *scratch):
    def done(g, real, imag, columns):
        a_ref[g, 0, :, :, columns] = real
        a_ref[g, 1, :, :, columns] = imag

    spectral_body(p_hbm, z_ref, w_ref, fold_ref, 1.0, o_ref, done, *scratch)


def backward_kernel(p_hbm, z_ref, w_ref, fold_ref, a_ref, o_ref, g_ref, *scratch):
    g_ref[...] = jnp.zeros_like(g_ref)

    def done(g, real, imag, columns):
        first, second = a_ref[g, 0, :, :, columns], a_ref[g, 1, :, :, columns]
        g_ref[0, :, :, columns] += first * real + second * imag
        g_ref[1, :, :, columns] += first * imag - second * real

    spectral_body(p_hbm, z_ref, w_ref, fold_ref, -1.0, o_ref, done, *scratch)

    for part in range(2):
        total = jnp.sum(g_ref[part], axis=1)
        rows = [total[:, b * 128 : b * 128 + 128] for b in range(LPAD // 128)]
        o_ref[:, GROUPS + part] = jnp.broadcast_to(
            jnp.concatenate(rows, axis=0).astype(BF16)[None], (LAT, JPAD, 128)
        )


def spectral_stage(kernel, blocks, tables, spectra, weights, fold, extra_in, extra_out, extra_scratch):
    whole = pl.BlockSpec(memory_space=pltpu.VMEM)
    return pl.pallas_call(
        kernel,
        out_shape=[pltpu.HBM((LAT, blocks, JPAD, 128), BF16)] + extra_out,
        in_specs=[pl.BlockSpec(memory_space=pl.ANY)] + [whole] * (3 + len(extra_in)),
        scratch_shapes=extra_scratch
        + [
            pltpu.VMEM((GROUPS * TG, 2, LHALF, JHALF), BF16),
            pltpu.VMEM((GROUPS, 2, JHALF, 128), F32),
            pltpu.SemaphoreType.DMA((GROUPS,)),
        ],
        compiler_params=params(52),
        cost_estimate=cost(1.2e10, 2.2e7),
        name="spectral_stage",
    )(tables, spectra, weights, hbm(fold), *[hbm(value) for value in extra_in])


def table_kernel(c1_ref, s1_ref, c2_ref, s2_ref, o_ref):
    @pl.loop(0, MUDIM // 128)
    def _(lc):
        lanes = pl.ds(pl.multiple_of(lc * 128, 128), 128)
        row = lax.broadcasted_iota(jnp.int32, (8, 128), 0)
        for start in range(NT):
            part = (row + 2 * start) % NT
            for pair in range(8):
                picked = []
                for n in (2 * pair, 2 * pair + 1):
                    for ref in (c2_ref, s2_ref):
                        rows = [
                            jnp.broadcast_to(ref[nt * 16 + n : nt * 16 + n + 1, lanes], (8, 128))
                            for nt in range(NT)
                        ]
                        picked.append(
                            jnp.where(part == 0, rows[0], jnp.where(part == 1, rows[1], rows[2]))
                        )
                for block in range(start, KDIM // 128, NT):
                    c1 = c1_ref[block * 8 : block * 8 + 8, lanes]
                    s1 = s1_ref[block * 8 : block * 8 + 8, lanes]
                    o_ref[block * 128 + pair * 16 : block * 128 + pair * 16 + 16, lanes] = (
                        jnp.concatenate(
                            [c1 * picked[0] - s1 * picked[1], c1 * picked[2] - s1 * picked[3]],
                            axis=0,
                        ).astype(BF16)
                    )


def fourier_table():
    mu = jnp.arange(MUDIM, dtype=jnp.int32)
    lat = mu // 128 * 2 + mu // 64 % 2
    wave = (lat + LAT * (mu // 16 % 4 * TG + mu % TG))[None, :]
    quarter = (mu // 8 % 2 * (POINTS // 4))[None, :]
    origin = (jnp.arange(LON * NT, dtype=jnp.int32) // NT * NLOC)[:, None]
    local = jnp.arange(NPAD, dtype=jnp.int32)[:, None]
    first = ((wave * origin + quarter) % POINTS).astype(F32) * (2.0 * math.pi / POINTS)
    second = (wave * local % POINTS).astype(F32) * (2.0 * math.pi / POINTS)
    table = pl.pallas_call(
        table_kernel,
        out_shape=pltpu.HBM((KDIM, MUDIM), BF16),
        compiler_params=params(32),
        cost_estimate=cost(1e7, 4e6),
        name="fourier_table",
    )(
        jnp.cos(first),
        jnp.sin(first),
        jnp.where(local < NLOC, jnp.cos(second), 0.0),
        jnp.where(local < NLOC, jnp.sin(second), 0.0),
    )
    return table, wave


def fold_matrix(lat):
    row = jnp.arange(JHALF, dtype=jnp.int32)[:, None]
    column = jnp.arange(JHALF, dtype=jnp.int32)[None, :]
    mirror = (column // JPAD == LAT // 2 - 1 - row // JPAD) & (
        column % JPAD == JLOC - 1 - row % JPAD
    )
    sign = jnp.where(lat % 2 == 0, 1.0, -1.0)
    return jnp.where(mirror, sign, 0.0).astype(BF16)


def swap(values, axis):
    return lax.all_to_all(values, axis, 0, 0, tiled=True)


def per_device(field, cotangent, spectral_filter):
    lat = lax.axis_index("lat")
    spacing = 2.0 * math.pi / POINTS
    table, wave = fourier_table()
    doubling = jnp.where(wave == 0, 1.0, 2.0).astype(F32)
    plain = jnp.ones((1, MUDIM), F32)
    theta = ((lat * JLOC + jnp.arange(JPAD)).astype(F32) + 0.5) * (math.pi / (JLOC * LAT))
    quadrature = jnp.broadcast_to(
        (spacing * math.pi / (JLOC * LAT) * jnp.sin(theta))[:, None], (JPAD, 128)
    )
    ones = jnp.ones((JPAD, 128), F32)
    low_tables = legendre_tables(lat, 0)
    weights = jnp.transpose(
        spectral_filter.astype(F32).reshape(2, DEG // 2, 2, CH), (0, 3, 2, 1)
    )
    weights = jnp.pad(weights, ((0, 0), (0, 0), (0, 0), (0, (LPAD - DEG) // 2)))
    weights = weights.reshape(2, CH, LPAD)
    fold = fold_matrix(lat)
    weights = jnp.broadcast_to(weights[:, :, None, :], (2, CH, TG, LPAD))

    field_shares = swap(to_shares(field), "lon")
    cot_local, table, low_tables = lax.optimization_barrier(
        (to_shares(cotangent), table, low_tables)
    )
    cot_shares = swap(cot_local, "lon")
    tables = legendre_tables(lat, HALF_GROUPS, low_tables)
    field_local, tables, fold, weights = lax.optimization_barrier(
        (to_waves(field_shares, table, quadrature, plain), tables, fold, weights)
    )
    field_waves = swap(field_local, "lat")
    cot_waves = swap(to_waves(cot_shares, table, ones, doubling), "lat")

    analysis_shape = (GROUPS, 2, CH, TG, LPAD)
    out_waves, analysis = spectral_stage(
        forward_kernel,
        GROUPS,
        tables,
        field_waves,
        weights,
        fold,
        [],
        [pltpu.HBM(analysis_shape, F32)],
        [],
    )
    (grad_waves,) = spectral_stage(
        backward_kernel,
        GROUPS + 2,
        tables,
        cot_waves,
        weights,
        fold,
        [analysis],
        [],
        [pltpu.VMEM((2, CH, TG, LPAD), F32)],
    )
    output_waves = swap(out_waves, "lat")
    grad_waves = swap(grad_waves, "lat")
    output = from_shares(swap(from_waves(output_waves, table, ones, doubling), "lon"))
    grad_field = from_shares(swap(from_waves(grad_waves, table, quadrature, plain), "lon"))
    summed = jnp.sum(grad_waves[:, GROUPS:].astype(F32), axis=0)
    summed = summed.reshape(2, LPAD // 128, CH, 128).transpose(0, 2, 1, 3)
    summed = summed.reshape(2, CH, 2, LHALF)[:, :, :, : DEG // 2]
    grad_filter = jnp.transpose(summed, (0, 3, 2, 1)).reshape(2, DEG, CH)
    return (output, grad_field, grad_filter)


def solution(mesh):
    in_specs = (P("lon", "lat", None), P("lon", "lat", None), P(None, None, "lon"))
    out_specs = (P("lon", "lat", None), P("lon", "lat", None), P(None, None, "lon"))
    return jax.shard_map(
        per_device, mesh=mesh, in_specs=in_specs, out_specs=out_specs, check_vma=False
    )
```
